32 devices in a mesh: grp: 4 (over x, core), mem: 8 (over z, y).
Axes of the slice: x: 2, y: 2, z: 4, core: 2. Of those that a mesh axis runs over, the one named last changes fastest.
Arguments:
- rhs: float32 [96, 448, 384], P('grp', 'mem'), may hold values from -6 to 6
- conductivity: float32 [96, 448], P('grp', 'mem'), may hold values from 0.2 to 5
- local_inverse: bfloat16 [65536, 2048], P(('grp', 'mem')), may hold values from -0.125 to 0.125
- coarse_basis: float32 [96, 448, 16], P('grp', 'mem'), may hold values from -0.5 to 0.5
- coarse_inverse: float32 [512, 512], P(('grp', 'mem')), may hold values from -3 to 8, as said below
Outputs:
- solution: float32 [96, 448, 384], P('grp', 'mem')
The draws below stay inside these ranges and needn't reach their ends.
Inputs may be any that keep to these rules, and one draw needn't show every extreme that they name: coarse_inverse is symmetric up to rounding, with a positive diagonal.
All inputs are finite; a program needn't handle non-finite values.
Results may differ from the reference program's by a relative error of at most 0.0005.
Values may be sent and summed in bfloat16 or wider, within the bound.
No kernel may reach another device: no remote copies, remote signals or barrier semaphores. Data moves between devices by JAX's collectives and lax.ppermute only.
A program may use at most 128 MiB of HBM per device.

```python
import math
import jax
import jax.numpy as jnp
from jax import lax

OX = 24
OY = 56
OV = 4
MODES = 16
RHS = 384
ITERS = 2
LOC = 2048
NC = 512
NX = 96
NY = 448
N_GRP = 4
N_MEM = 8


def draw_coarse_inverse(key, part):
    base = jax.random.normal(jax.random.fold_in(key, 11), (NC, NC), jnp.float32) * (0.5 / math.sqrt(NC))
    symmetric = base + base.T + jnp.eye(NC, dtype=jnp.float32)
    return symmetric


def block_levels(rng, dims, cuts, smallest, high):
    loudness, own = 1.0, jax.random.fold_in(rng, 6)
    for dim, blocks in cuts:
        heights = jnp.exp(jax.random.uniform(jax.random.fold_in(own, dim), (blocks,), jnp.float32, smallest / len(cuts), high / len(cuts)))
        loudness = loudness * jnp.repeat(heights, dims[dim] // blocks).reshape([-1 if axis == dim else 1 for axis in range(len(dims))])
    return loudness


def scatter_about(stream_key, dims, width, reach, shards=(), kind=jnp.bfloat16):
    loudness = block_levels(stream_key, dims, shards, -0.22, 0.18) if shards else 1.0
    entries = jax.random.normal(stream_key, dims, jnp.float32) * width * loudness
    return jnp.minimum(jnp.maximum(entries, -reach), reach).astype(kind)


def setup_inputs(seed: int = 0) -> dict:
    arg_keys = jax.random.split(jax.random.key(seed), 6)
    rhs = scatter_about(arg_keys[0], (NX, NY, RHS), 1.0, 6.0, ((0, 4), (1, 8)), jnp.float32)
    conductivity = jnp.clip(jnp.exp(math.log(5.0) - 3.218876 * jax.random.uniform(arg_keys[1], (NX, NY), jnp.float32) ** block_levels(arg_keys[1], (NX, NY), ((0, 4), (1, 8)), -0.2, 0.2)), 0.2, 5.0)
    local_inverse = scatter_about(arg_keys[2], (N_GRP * N_MEM * LOC, LOC), LOC ** -0.5, 0.125, ((0, 32),))
    coarse_basis = scatter_about(arg_keys[3], (NX, NY, MODES), (OX * OY // 8) ** -0.5, 0.5, ((0, 4), (1, 8)), jnp.float32)
    coarse_inverse = draw_coarse_inverse(jax.random.fold_in(arg_keys[5], 71), 0)
    return dict(rhs=rhs, conductivity=conductivity, local_inverse=local_inverse, coarse_basis=coarse_basis, coarse_inverse=coarse_inverse)


def apply_operator(field_pad, conduct_pad):
    center = field_pad[1:-1, 1:-1]
    conduct_mid = conduct_pad[1:-1, 1:-1]
    neighbour_fields = (field_pad[2:, 1:-1], field_pad[:-2, 1:-1], field_pad[1:-1, 2:], field_pad[1:-1, :-2])
    neighbour_conduct = (conduct_pad[2:, 1:-1], conduct_pad[:-2, 1:-1], conduct_pad[1:-1, 2:], conduct_pad[1:-1, :-2])
    summed = jnp.zeros(center.shape, jnp.float32)
    for other_field, other_conduct in zip(neighbour_fields, neighbour_conduct):
        face = 0.5 * (conduct_mid + other_conduct)
        summed = summed + face[:, :, None] * (center - other_field)
    return summed


def reference(rhs, conductivity, local_inverse, coarse_basis, coarse_inverse):
    groups = N_GRP
    members = N_MEM
    span_x = OX + 2 * OV
    span_y = OY + 2 * OV
    conduct_pad = jnp.pad(conductivity, 1)
    solution = jnp.zeros(rhs.shape, jnp.float32)
    basis_five = coarse_basis.reshape(groups, OX, members, OY, MODES)
    for sweep in range(ITERS):
        solution_pad = jnp.pad(solution, ((1, 1), (1, 1), (0, 0)))
        residual = rhs - apply_operator(solution_pad, conduct_pad)
        residual_pad = jnp.pad(residual, ((OV, OV), (OV, OV), (0, 0)))

        def local_solve(subdomain):
            group_index = subdomain // members
            member_index = subdomain % members
            zero_start = jnp.zeros((), jnp.int32)
            extended = lax.dynamic_slice(residual_pad, (group_index * OX, member_index * OY, zero_start), (span_x, span_y, RHS))
            flat_rows = extended.reshape(LOC, RHS).astype(jnp.bfloat16)
            inverse_block = lax.dynamic_slice_in_dim(local_inverse, subdomain * LOC, LOC, 0)
            product = jnp.dot(inverse_block, flat_rows, preferred_element_type=jnp.float32)
            return product.reshape(span_x, span_y, RHS)[OV:OV + OX, OV:OV + OY]

        fine_blocks = lax.map(local_solve, jnp.arange(groups * members, dtype=jnp.int32))
        fine_part = fine_blocks.reshape(groups, members, OX, OY, RHS).transpose(0, 2, 1, 3, 4).reshape(NX, NY, RHS)
        residual_five = residual.reshape(groups, OX, members, OY, RHS)
        restricted = jnp.einsum('gxmyk,gxmyr->gmkr', basis_five, residual_five, precision=lax.Precision.HIGHEST).reshape(NC, RHS)
        lifted = jnp.dot(coarse_inverse, restricted, precision=lax.Precision.HIGHEST, preferred_element_type=jnp.float32)
        lifted = lifted.reshape(groups, members, MODES, RHS)
        coarse_part = jnp.einsum('gxmyk,gmkr->gxmyr', basis_five, lifted, precision=lax.Precision.HIGHEST).reshape(NX, NY, RHS)
        solution = solution + fine_part + coarse_part
    return solution
```

```python
import jax
import jax.numpy as jnp
from jax import lax
from jax.sharding import PartitionSpec as P

OV = 4
ITERS = 2
AXES = ("grp", "mem")
EXACT = lax.Precision.HIGHEST


def neighbour_pairs(count, first):
    pairs = [(i, i + 1) for i in range(first, count - 1, 2)]
    return pairs + [(j, i) for i, j in pairs]


def edges(low_edge, high_edge, axis):
    count = lax.axis_size(axis)
    even = lax.axis_index(axis) % 2 == 0
    first = lax.ppermute(
        jnp.where(even, high_edge, low_edge), axis, neighbour_pairs(count, 0)
    )
    second = lax.ppermute(
        jnp.where(even, low_edge, high_edge), axis, neighbour_pairs(count, 1)
    )
    return jnp.where(even, second, first), jnp.where(even, first, second)


def dim_edges(block, axis, dim, width):
    size = block.shape[dim]
    low_edge = lax.slice_in_dim(block, 0, width, axis=dim)
    high_edge = lax.slice_in_dim(block, size - width, size, axis=dim)
    return edges(low_edge, high_edge, axis)


def padded(block, axis, dim, width):
    low, high = dim_edges(block, axis, dim, width)
    return jnp.concatenate([low, block, high], axis=dim)


def power_of_two(count):
    return count & (count - 1) == 0


def masks():
    members, groups = lax.axis_size("mem"), lax.axis_size("grp")
    mem_bits = [1 << k for k in range(members.bit_length() - 1)]
    grp_bits = [members << k for k in range(groups.bit_length() - 1)]
    return mem_bits[:0:-1] + grp_bits[:1], mem_bits[:1] + grp_bits[1:]


def swap(value, bit):
    total = lax.axis_size("grp") * lax.axis_size("mem")
    return lax.ppermute(value, AXES, [(i, i ^ bit) for i in range(total)])


def gathered(value, bits):
    for bit in bits:
        value = jnp.concatenate([value, swap(value, bit)], axis=0)
    return value


def coarse_solve(inverse_rows, restricted, modes):
    gather_bits, sum_bits = masks()
    sources = gathered(restricted, gather_bits)
    shares = lax.dot_general(
        inverse_rows,
        sources,
        (((0,), (0,)), ((), ())),
        precision=EXACT,
        preferred_element_type=jnp.float32,
    )
    me = lax.axis_index(AXES)
    targets = [0]
    for bit in sum_bits[::-1]:
        targets = targets + [t ^ bit for t in targets]
    parts = [
        lax.dynamic_slice_in_dim(shares, (me ^ target) * modes, modes, 0) for target in targets
    ]
    for bit in sum_bits:
        half = len(parts) // 2
        got = swap(jnp.concatenate(parts[half:], axis=0), bit)
        parts = [
            part + got[k * modes : (k + 1) * modes] for k, part in enumerate(parts[:half])
        ]
    return parts[0]


def on_device(rhs, conductivity, local_inverse, coarse_basis, coarse_inverse):
    own_x, own_y, columns = rhs.shape
    modes = coarse_basis.shape[2]
    span_x = own_x + 2 * OV
    span_y = own_y + 2 * OV
    cells = own_x * own_y
    owned_inverse = local_inverse[OV * span_y : (OV + own_x) * span_y]
    basis_flat = coarse_basis.reshape(cells, modes)

    below, above = dim_edges(conductivity, "grp", 0, 1)
    left, right = dim_edges(conductivity, "mem", 1, 1)
    conduct_x = jnp.concatenate([below, conductivity, above], axis=0)
    conduct_y = jnp.concatenate([left, conductivity, right], axis=1)
    faces_x = 0.5 * (conduct_x[1:] + conduct_x[:-1])[:, :, None]
    faces_y = 0.5 * (conduct_y[:, 1:] + conduct_y[:, :-1])[:, :, None]

    def residual_of(solution):
        along_x = padded(solution, "grp", 0, 1)
        along_y = padded(solution, "mem", 1, 1)
        summed = faces_x[1:] * (solution - along_x[2:])
        summed = summed + faces_x[:-1] * (solution - along_x[:-2])
        summed = summed + faces_y[:, 1:] * (solution - along_y[:, 2:])
        summed = summed + faces_y[:, :-1] * (solution - along_y[:, :-2])
        return rhs - summed

    def fine(residual):
        extended = padded(residual.astype(jnp.bfloat16), "grp", 0, OV)
        extended = padded(extended, "mem", 1, OV)
        product = jnp.dot(
            owned_inverse,
            extended.reshape(span_x * span_y, columns),
            preferred_element_type=jnp.float32,
        )
        return product.reshape(own_x, span_y, columns)[:, OV : OV + own_y]

    inverse_rows = gathered(coarse_inverse, masks()[0])

    def coarse(residual):
        restricted = lax.dot_general(
            basis_flat,
            residual.reshape(cells, columns),
            (((0,), (0,)), ((), ())),
            precision=EXACT,
            preferred_element_type=jnp.float32,
        )
        lifted = coarse_solve(inverse_rows, restricted, modes)
        return jnp.dot(
            basis_flat, lifted, precision=EXACT, preferred_element_type=jnp.float32
        ).reshape(own_x, own_y, columns)

    solution = fine(rhs) + coarse(rhs)
    for sweep in range(ITERS - 1):
        residual = residual_of(solution)
        solution = solution + fine(residual) + coarse(residual)
    return solution


def solution(mesh):
    placed = (
        P("grp", "mem", None),
        P("grp", "mem"),
        P(("grp", "mem"), None),
        P("grp", "mem", None),
        P(("grp", "mem"), None),
    )
    return jax.shard_map(
        on_device, mesh=mesh, in_specs=placed, out_specs=P("grp", "mem", None), check_vma=False
    )
```

```python
import functools

import jax
import jax.numpy as jnp
from jax import lax
from jax.experimental import pallas as pl
from jax.experimental.pallas import tpu as pltpu
from jax.sharding import PartitionSpec as P

OV = 4
ITERS = 2
LANES = 128
AXES = ("grp", "mem")
EXACT = lax.Precision.HIGHEST
F32 = jnp.float32
BF16 = jnp.bfloat16


def neighbour_pairs(count, first):
    pairs = [(i, i + 1) for i in range(first, count - 1, 2)]
    return pairs + [(j, i) for i, j in pairs]


def edges(low_edge, high_edge, axis):
    count = lax.axis_size(axis)
    even = lax.axis_index(axis) % 2 == 0
    first = lax.ppermute(jnp.where(even, high_edge, low_edge), axis, neighbour_pairs(count, 0))
    second = lax.ppermute(jnp.where(even, low_edge, high_edge), axis, neighbour_pairs(count, 1))
    return jnp.where(even, second, first), jnp.where(even, first, second)


def masks():
    members, groups = lax.axis_size("mem"), lax.axis_size("grp")
    mem_bits = [1 << k for k in range(members.bit_length() - 1)]
    grp_bits = [members << k for k in range(groups.bit_length() - 1)]
    return mem_bits[:0:-1] + grp_bits[:1], mem_bits[:1] + grp_bits[1:]


def swap(value, bit):
    total = lax.axis_size("grp") * lax.axis_size("mem")
    return lax.ppermute(value, AXES, [(i, i ^ bit) for i in range(total)])


def gathered(value, bits):
    for bit in bits:
        value = jnp.concatenate([value, swap(value, bit)], axis=0)
    return value


def summed_shares(inverse_rows, sources, modes):
    shares = lax.dot_general(
        inverse_rows,
        sources,
        (((0,), (0,)), ((), ())),
        precision=EXACT,
        preferred_element_type=F32,
    )
    sum_bits = masks()[1]
    me = lax.axis_index(AXES)
    targets = [0]
    for bit in sum_bits[::-1]:
        targets = targets + [t ^ bit for t in targets]
    parts = [
        lax.dynamic_slice_in_dim(shares, (me ^ target) * modes, modes, 0) for target in targets
    ]
    for bit in sum_bits:
        half = len(parts) // 2
        got = swap(jnp.concatenate(parts[half:], axis=0), bit)
        parts = [part + got[k * modes : (k + 1) * modes] for k, part in enumerate(parts[:half])]
    return parts[0]


def survey(block, basis, step, low_ref, high_ref, side_ref, sum_ref):
    rows, own_y, columns = block.shape

    @pl.when(step == 0)
    def _():
        low_ref[...] = block.astype(BF16)
        sum_ref[...] = jnp.zeros_like(sum_ref)

    @pl.when(step == pl.num_programs(0) - 1)
    def _():
        high_ref[...] = block.astype(BF16)

    first = lax.broadcasted_iota(jnp.int32, (rows, 2 * OV, columns), 1) < OV
    side_ref[...] = jnp.where(first, block[:, : 2 * OV], block[:, own_y - 2 * OV :]).astype(BF16)
    sum_ref[...] += lax.dot_general(
        basis,
        block.reshape(rows * own_y, columns),
        (((0,), (0,)), ((), ())),
        precision=EXACT,
        preferred_element_type=F32,
    )


def start_kernel(block_ref, basis_ref, low_ref, high_ref, side_ref, sum_ref):
    survey(
        block_ref[...], basis_ref[...], pl.program_id(0), low_ref, high_ref, side_ref, sum_ref
    )


def residual_kernel(
    rhs_ref,
    now_ref,
    before_ref,
    after_ref,
    below_ref,
    above_ref,
    left_ref,
    right_ref,
    heat_ref,
    heat_before_ref,
    heat_after_ref,
    basis_ref,
    out_ref,
    low_ref,
    high_ref,
    side_ref,
    sum_ref,
):
    step = pl.program_id(0)
    last = pl.num_programs(0) - 1
    rows, own_y, columns = now_ref.shape
    wide = columns + LANES

    def spread(heat):
        return jnp.concatenate([heat] * (columns // LANES), axis=1)

    def row(index):
        return jnp.concatenate([now_ref[index], heat_ref[index]], axis=1)

    before = jnp.concatenate([before_ref[0], heat_before_ref[0]], axis=1)
    after = jnp.concatenate([after_ref[0], heat_after_ref[0]], axis=1)
    before = jnp.where(step == 0, below_ref[0], before)
    after = jnp.where(step == last, above_ref[0], after)
    place = lax.broadcasted_iota(jnp.int32, (own_y, wide), 0)
    for index in range(rows):
        here = row(index)
        up = row(index + 1) if index + 1 < rows else after
        down = row(index - 1) if index else before
        right = jnp.where(
            place == own_y - 1, right_ref[0, index : index + 1], pltpu.roll(here, own_y - 1, 0)
        )
        left = jnp.where(place == 0, left_ref[0, index : index + 1], pltpu.roll(here, 1, 0))
        summed = jnp.zeros((own_y, columns), F32)
        for other in (up, down, right, left):
            face = 0.5 * (here[:, columns:] + other[:, columns:])
            summed = summed + spread(face) * (here[:, :columns] - other[:, :columns])
        out_ref[index] = rhs_ref[index] - summed
    survey(out_ref[...], basis_ref[...], step, low_ref, high_ref, side_ref, sum_ref)


def fine_kernel(
    has_base,
    inverse_ref,
    block_ref,
    low_ref,
    high_ref,
    side_ref,
    basis_ref,
    lifted_ref,
    *refs,
):
    if has_base:
        base_ref, out_ref, window, wide, product = refs
    else:
        heat_ref, out_ref, first_ref, last_ref, left_ref, right_ref, window, wide, product = refs
    step = pl.program_id(0)
    own_x, own_y, columns = block_ref.shape
    span_y = own_y + 2 * OV
    rows = out_ref.shape[0]

    @pl.when(step == 0)
    def _():
        def place(index, values):
            wide[OV : OV + own_y, :] = values
            sides = side_ref[index].astype(F32)
            wide[:OV, :] = sides[:OV]
            wide[OV + own_y :, :] = sides[OV:]
            start = index * span_y
            if not isinstance(index, int):
                start = pl.multiple_of(start, span_y)
            window[pl.ds(start, span_y), :] = wide[...].astype(BF16)

        for index in range(OV):
            place(index, low_ref[index].astype(F32))
            place(OV + own_x + index, high_ref[index].astype(F32))

        @pl.loop(0, own_x, unroll=4)
        def _(index):
            place(OV + index, block_ref[index])

    product[...] = jnp.dot(inverse_ref[...], window[...], preferred_element_type=F32)
    coarse = jnp.dot(basis_ref[...], lifted_ref[...], precision=EXACT, preferred_element_type=F32)
    for index in range(rows):
        value = product[index * span_y + OV : index * span_y + OV + own_y, :]
        value = value + coarse[index * own_y : (index + 1) * own_y]
        if has_base:
            value = base_ref[index] + value
        out_ref[index] = value
    if not has_base:
        final = pl.num_programs(0) - 1

        @pl.when(step == 0)
        def _():
            first_ref[0] = jnp.concatenate([out_ref[0], heat_ref[0]], axis=1)

        @pl.when(step == final)
        def _():
            last_ref[0] = jnp.concatenate([out_ref[rows - 1], heat_ref[rows - 1]], axis=1)

        for index in range(rows):
            for ref, at in ((left_ref, 0), (right_ref, own_y - 1)):
                ref[0, index : index + 1, :columns] = out_ref[index, at : at + 1]
                ref[0, index : index + 1, columns:] = heat_ref[index, at : at + 1]


def whole(shape):
    return pl.BlockSpec(shape, lambda i: (0,) * len(shape))


def tiles(shape):
    return pl.BlockSpec(shape, lambda i: (i,) + (0,) * (len(shape) - 1))


def shape_of(shape, kind):
    return jax.ShapeDtypeStruct(shape, kind)


def on_device(rhs, conductivity, local_inverse, coarse_basis, coarse_inverse):
    own_x, own_y, columns = rhs.shape
    modes = coarse_basis.shape[2]
    span_x = own_x + 2 * OV
    span_y = own_y + 2 * OV
    local = span_x * span_y
    cells = own_x * own_y
    steps = own_x // OV
    basis_flat = coarse_basis.reshape(cells, modes)
    heat = jnp.broadcast_to(conductivity[:, :, None], (own_x, own_y, LANES))
    params = pltpu.CompilerParams(vmem_limit_bytes=32 * 2**20)

    block = (OV, own_y, columns)
    basis_block = tiles((OV * own_y, modes))
    survey_shapes = [
        shape_of(block, BF16),
        shape_of(block, BF16),
        shape_of((own_x, 2 * OV, columns), BF16),
        shape_of((modes, columns), F32),
    ]
    survey_specs = [
        whole(block),
        whole(block),
        tiles((OV, 2 * OV, columns)),
        whole((modes, columns)),
    ]

    def surveyed_start():
        return pl.pallas_call(
            start_kernel,
            grid=(steps,),
            in_specs=[tiles(block), basis_block],
            out_specs=survey_specs,
            out_shape=survey_shapes,
            compiler_params=params,
        )(rhs, basis_flat)

    def surveyed_residual(now, around):
        below, above, left, right = around

        def before(size):
            return pl.BlockSpec((1, own_y, size), lambda i: (jnp.maximum(i * OV - 1, 0), 0, 0))

        def after(size):
            return pl.BlockSpec(
                (1, own_y, size), lambda i: (jnp.minimum(i * OV + OV, own_x - 1), 0, 0)
            )

        edge = columns + LANES
        return pl.pallas_call(
            residual_kernel,
            grid=(steps,),
            in_specs=[
                tiles(block),
                tiles(block),
                before(columns),
                after(columns),
                whole((1, own_y, edge)),
                whole((1, own_y, edge)),
                tiles((1, OV, edge)),
                tiles((1, OV, edge)),
                tiles((OV, own_y, LANES)),
                before(LANES),
                after(LANES),
                basis_block,
            ],
            out_specs=[tiles(block)] + survey_specs,
            out_shape=[shape_of(rhs.shape, F32)] + survey_shapes,
            compiler_params=params,
        )(rhs, now, now, now, below, above, left, right, heat, heat, heat, basis_flat)

    def window_margins(low_edge, high_edge, sides):
        low, high = edges(low_edge, high_edge, "grp")
        corners = [jnp.concatenate([m[:, :OV], m[:, -OV:]], axis=1) for m in (low, high)]
        sides = jnp.concatenate([corners[0], sides, corners[1]], axis=0)
        left, right = edges(sides[:, :OV], sides[:, OV:], "mem")
        return low, high, jnp.concatenate([left, right], axis=1)

    def improved(values, margins, lifted, now):
        low, high, sides = margins
        edge = columns + LANES
        in_specs = [
            pl.BlockSpec((OV * span_y, local), lambda i: (i + 1, 0)),
            whole(rhs.shape),
            whole(block),
            whole(block),
            whole((span_x, 2 * OV, columns)),
            basis_block,
            whole((modes, columns)),
        ]
        out_specs = [tiles(block)]
        out_shape = [shape_of(rhs.shape, F32)]
        if now is None:
            in_specs.append(tiles((OV, own_y, LANES)))
            out_specs += [whole((1, own_y, edge))] * 2 + [tiles((1, OV, edge))] * 2
            out_shape += [shape_of((1, own_y, edge), F32)] * 2
            out_shape += [shape_of((steps, OV, edge), F32)] * 2
        else:
            in_specs.append(tiles(block))
        return pl.pallas_call(
            functools.partial(fine_kernel, now is not None),
            grid=(steps,),
            in_specs=in_specs,
            out_specs=out_specs,
            out_shape=out_shape,
            scratch_shapes=[
                pltpu.VMEM((local, columns), BF16),
                pltpu.VMEM((span_y, columns), F32),
                pltpu.VMEM((OV * span_y, columns), F32),
            ],
            compiler_params=params,
        )(
            local_inverse,
            values,
            low,
            high,
            sides,
            basis_flat,
            lifted,
            heat if now is None else now,
        )

    gather_bits = masks()[0]
    *to_send, restricted = surveyed_start()
    sources = gathered(jnp.concatenate([restricted, coarse_inverse], axis=1), gather_bits)
    inverse_rows = sources[:, columns:]
    margins = window_margins(*to_send)
    lifted = summed_shares(inverse_rows, sources[:, :columns], modes)
    now, first, final, left, right = improved(rhs, margins, lifted, None)
    for sweep in range(ITERS - 1):
        around = edges(first, final, "grp") + edges(left, right, "mem")
        residual, *to_send, restricted = surveyed_residual(now, around)
        sources = gathered(restricted, gather_bits)
        margins = window_margins(*to_send)
        lifted = summed_shares(inverse_rows, sources, modes)
        now = improved(residual, margins, lifted, now)[0]
    return now


def solution(mesh):
    placed = (
        P("grp", "mem", None),
        P("grp", "mem"),
        P(("grp", "mem"), None),
        P("grp", "mem", None),
        P(("grp", "mem"), None),
    )
    return jax.shard_map(
        on_device, mesh=mesh, in_specs=placed, out_specs=P("grp", "mem", None), check_vma=False
    )
```

```python
import functools

import jax
import jax.numpy as jnp
from jax import lax
from jax.experimental import pallas as pl
from jax.experimental.pallas import tpu as pltpu
from jax.sharding import PartitionSpec as P

OV = 4
ITERS = 2
LANES = 128
AXES = ("grp", "mem")
EXACT = lax.Precision.HIGHEST
F32 = jnp.float32
BF16 = jnp.bfloat16


def neighbour_pairs(count, first):
    pairs = [(i, i + 1) for i in range(first, count - 1, 2)]
    return pairs + [(j, i) for i, j in pairs]


def edges(low_edge, high_edge, axis):
    count = lax.axis_size(axis)
    even = lax.axis_index(axis) % 2 == 0
    first = lax.ppermute(jnp.where(even, high_edge, low_edge), axis, neighbour_pairs(count, 0))
    second = lax.ppermute(jnp.where(even, low_edge, high_edge), axis, neighbour_pairs(count, 1))
    return jnp.where(even, second, first), jnp.where(even, first, second)


def masks():
    members, groups = lax.axis_size("mem"), lax.axis_size("grp")
    mem_bits = [1 << k for k in range(members.bit_length() - 1)]
    grp_bits = [members << k for k in range(groups.bit_length() - 1)]
    return mem_bits[:0:-1] + grp_bits[:1], mem_bits[:1] + grp_bits[1:]


def swap(value, bit):
    total = lax.axis_size("grp") * lax.axis_size("mem")
    return lax.ppermute(value, AXES, [(i, i ^ bit) for i in range(total)])


def gathered(value, bits):
    for bit in bits:
        value = jnp.concatenate([value, swap(value, bit)], axis=0)
    return value


def summed_shares(inverse_rows, sources, modes):
    shares = lax.dot_general(
        inverse_rows,
        sources,
        (((0,), (0,)), ((), ())),
        precision=EXACT,
        preferred_element_type=F32,
    )
    sum_bits = masks()[1]
    me = lax.axis_index(AXES)
    targets = [0]
    for bit in sum_bits[::-1]:
        targets = targets + [t ^ bit for t in targets]
    parts = [
        lax.dynamic_slice_in_dim(shares, (me ^ target) * modes, modes, 0) for target in targets
    ]
    for bit in sum_bits:
        half = len(parts) // 2
        got = swap(jnp.concatenate(parts[half:], axis=0), bit)
        parts = [part + got[k * modes : (k + 1) * modes] for k, part in enumerate(parts[:half])]
    return parts[0]


def split(values):
    high = values.astype(BF16)
    rest = values - high.astype(F32)
    middle = rest.astype(BF16)
    return high, middle, (rest - middle.astype(F32)).astype(BF16)


def product(a, b):
    return jnp.dot(a, b, preferred_element_type=F32)


def modes_of(basis_ref, first, rows):
    return split(jnp.concatenate([basis_ref[first + k] for k in range(rows)], axis=1))


def restrict(basis_ref, first, block):
    rows, own_y, columns = block.shape
    high, middle, low = modes_of(basis_ref, first, rows)
    modes = high.shape[0]
    block_high, block_middle, block_low = split(block.reshape(rows * own_y, columns))
    three = product(jnp.concatenate([high, middle, low], axis=0), block_high)
    two = product(jnp.concatenate([high, middle], axis=0), block_middle)
    one = product(high, block_low)
    return one + (two[modes:] + three[2 * modes :]) + (two[:modes] + three[modes : 2 * modes]) + three[:modes]


def survey(block, basis_ref, first, low_ref, high_ref, side_ref):
    rows, own_y, columns = block.shape
    if first == 0:
        low_ref[...] = block[:OV].astype(BF16)
    if first + rows == side_ref.shape[0]:
        high_ref[...] = block[rows - OV :].astype(BF16)
    left = lax.broadcasted_iota(jnp.int32, (rows, 2 * OV, columns), 1) < OV
    side_ref[first : first + rows] = jnp.where(
        left, block[:, : 2 * OV], block[:, own_y - 2 * OV :]
    ).astype(BF16)
    return restrict(basis_ref, first, block)


def start_kernel(rhs_ref, basis_ref, low_ref, high_ref, side_ref, sum_ref, held, arrived):
    own_x = held.shape[0]
    copies = [
        pltpu.make_async_copy(
            rhs_ref.at[pl.ds(first, OV)], held.at[pl.ds(first, OV)], arrived.at[first // OV]
        )
        for first in range(0, own_x, OV)
    ]
    for copy in copies:
        copy.start()
    total = jnp.zeros(sum_ref.shape, F32)
    for first in range(0, own_x, OV):
        copies[first // OV].wait()
        block = held[first : first + OV]
        total = total + survey(block, basis_ref, first, low_ref, high_ref, side_ref)
    sum_ref[...] = total


def residual_kernel(
    rhs_ref,
    now_ref,
    below_ref,
    above_ref,
    left_ref,
    right_ref,
    heat_ref,
    basis_ref,
    out_ref,
    low_ref,
    high_ref,
    side_ref,
    sum_ref,
):
    own_x, own_y, columns = now_ref.shape
    place = lax.broadcasted_iota(jnp.int32, (own_y, columns), 0)
    place_heat = place[:, :LANES]

    def flux(values, heat, other, other_heat):
        face = 0.5 * (heat + other_heat)
        return jnp.concatenate([face] * (columns // LANES), axis=1) * (values - other)

    def parts(row):
        return row[:, :columns], row[:, columns:]

    here, heat = now_ref[0], heat_ref[0]
    before = flux(*parts(below_ref[0]), here, heat)
    total = jnp.zeros(sum_ref.shape, F32)
    for index in range(own_x):
        if index + 1 < own_x:
            after, after_heat = now_ref[index + 1], heat_ref[index + 1]
        else:
            after, after_heat = parts(above_ref[0])
        across = flux(here, heat, after, after_heat)
        right, right_heat = parts(right_ref[index // OV, index % OV : index % OV + 1])
        left, left_heat = parts(left_ref[index // OV, index % OV : index % OV + 1])
        right = jnp.where(place == own_y - 1, right, pltpu.roll(here, own_y - 1, 0))
        right_heat = jnp.where(place_heat == own_y - 1, right_heat, pltpu.roll(heat, own_y - 1, 0))
        along = flux(here, heat, right, right_heat)
        entering = jnp.where(
            place == 0, flux(left, left_heat, here[:1], heat[:1]), pltpu.roll(along, 1, 0)
        )
        out_ref[index] = rhs_ref[index] - ((across - before) + (along - entering))
        here, heat, before = after, after_heat, across
        if index % OV == OV - 1:
            first = index + 1 - OV
            block = out_ref[first : first + OV]
            total = total + survey(block, basis_ref, first, low_ref, high_ref, side_ref)
    sum_ref[...] = total


def fine_kernel(
    last,
    inverse_ref,
    block_ref,
    low_ref,
    high_ref,
    side_ref,
    basis_ref,
    lifted_ref,
    extra_ref,
    out_ref,
    *refs,
):
    if last:
        rows_held, window, wide, solved, arrived, result, left_for = refs
    else:
        first_ref, last_ref, left_ref, right_ref, rows_held, window, wide, solved, arrived = refs
        result = out_ref
    own_x, own_y, columns = block_ref.shape
    span_y = own_y + 2 * OV
    rows = solved.shape[0] // span_y
    copies = []
    for first in range(0, own_x, rows):
        count = rows * span_y
        copies.append(
            pltpu.make_async_copy(
                inverse_ref.at[pl.ds((OV + first) * span_y, count)],
                rows_held.at[pl.ds(first * span_y, count)],
                arrived.at[first // rows],
            )
        )
        copies[-1].start()

    def place(index, values):
        wide[OV : OV + own_y, :] = values
        sides = side_ref[index].astype(F32)
        wide[:OV, :] = sides[:OV]
        wide[OV + own_y :, :] = sides[OV:]
        window[index * span_y : (index + 1) * span_y, :] = wide[...].astype(BF16)

    for index in range(OV):
        place(index, low_ref[index].astype(F32))
        place(OV + own_x + index, high_ref[index].astype(F32))
    for index in range(own_x):
        place(OV + index, block_ref[index])

    high, middle, low = split(lifted_ref[...])
    lifted = jnp.concatenate([high, middle, high, low, middle, high], axis=0)
    sends = []
    for first in range(0, own_x, rows):
        copies[first // rows].wait()
        solved[...] = product(
            rows_held[first * span_y : (first + rows) * span_y, :], window[...]
        )
        high, middle, low = modes_of(basis_ref, first, rows)
        coarse = lax.dot_general(
            jnp.concatenate([high, high, middle, high, middle, low], axis=0),
            lifted,
            (((0,), (0,)), ((), ())),
            preferred_element_type=F32,
        )
        for k in range(rows):
            value = solved[k * span_y + OV : k * span_y + OV + own_y, :]
            value = value + coarse[k * own_y : (k + 1) * own_y]
            if last:
                value = extra_ref[first + k] + value
            result[first + k] = value
        if last:
            sends.append(
                pltpu.make_async_copy(
                    result.at[pl.ds(first, rows)],
                    out_ref.at[pl.ds(first, rows)],
                    left_for.at[first // rows],
                )
            )
            sends[-1].start()
        else:
            for index in range(first, first + rows):
                for ref, at in ((left_ref, 0), (right_ref, own_y - 1)):
                    row = pl.ds(index % OV, 1)
                    ref[index // OV, row, :columns] = result[index, at : at + 1]
                    ref[index // OV, row, columns:] = extra_ref[index, at : at + 1]
    for send in sends:
        send.wait()
    if not last:
        first_ref[0] = jnp.concatenate([result[0], extra_ref[0]], axis=1)
        last_ref[0] = jnp.concatenate([result[own_x - 1], extra_ref[own_x - 1]], axis=1)


def shape_of(shape, kind):
    return jax.ShapeDtypeStruct(shape, kind)


def on_device(rhs, conductivity, local_inverse, coarse_basis, coarse_inverse):
    own_x, own_y, columns = rhs.shape
    modes = coarse_basis.shape[2]
    span_x = own_x + 2 * OV
    span_y = own_y + 2 * OV
    local = span_x * span_y
    basis = jnp.transpose(coarse_basis, (0, 2, 1))
    heat = jnp.broadcast_to(conductivity[:, :, None], (own_x, own_y, LANES))
    params = pltpu.CompilerParams(vmem_limit_bytes=40 * 2**20)
    group = 2 * OV if own_x % (2 * OV) == 0 else OV
    in_vmem = pl.BlockSpec(memory_space=pltpu.VMEM)
    in_hbm = pl.BlockSpec(memory_space=pltpu.HBM)

    survey_shapes = [
        shape_of((OV, own_y, columns), BF16),
        shape_of((OV, own_y, columns), BF16),
        shape_of((own_x, 2 * OV, columns), BF16),
        shape_of((modes, columns), F32),
    ]

    def surveyed_start():
        return pl.pallas_call(
            start_kernel,
            in_specs=[in_hbm, in_vmem],
            out_specs=[in_vmem] * 4,
            out_shape=survey_shapes,
            scratch_shapes=[
                pltpu.VMEM(rhs.shape, F32),
                pltpu.SemaphoreType.DMA((own_x // OV,)),
            ],
            compiler_params=params,
        )(rhs, basis)

    def surveyed_residual(now, around):
        return pl.pallas_call(
            residual_kernel,
            in_specs=[in_vmem] * 8,
            out_specs=[in_vmem] * 5,
            out_shape=[shape_of(rhs.shape, F32)] + survey_shapes,
            compiler_params=params,
        )(rhs, now, *around, heat, basis)

    def window_margins(low_edge, high_edge, sides):
        low, high = edges(low_edge, high_edge, "grp")
        corners = [jnp.concatenate([m[:, :OV], m[:, -OV:]], axis=1) for m in (low, high)]
        sides = jnp.concatenate([corners[0], sides, corners[1]], axis=0)
        left, right = edges(sides[:, :OV], sides[:, OV:], "mem")
        return low, high, jnp.concatenate([left, right], axis=1)

    def improved(values, margins, lifted, now):
        last = now is not None
        edge = columns + LANES
        out_shape = [shape_of(rhs.shape, F32)]
        scratch = [
            pltpu.VMEM((own_x * span_y, local), BF16),
            pltpu.VMEM((local, columns), BF16),
            pltpu.VMEM((span_y, columns), F32),
            pltpu.VMEM((group * span_y, columns), F32),
            pltpu.SemaphoreType.DMA((own_x // group,)),
        ]
        if last:
            out_specs = [in_hbm]
            scratch += [pltpu.VMEM(rhs.shape, F32), pltpu.SemaphoreType.DMA((own_x // group,))]
        else:
            out_specs = [in_vmem] * 5
            out_shape += [shape_of((1, own_y, edge), F32)] * 2
            out_shape += [shape_of((own_x // OV, OV, edge), F32)] * 2
        return pl.pallas_call(
            functools.partial(fine_kernel, last),
            in_specs=[in_hbm] + [in_vmem] * 7,
            out_specs=out_specs,
            out_shape=out_shape,
            scratch_shapes=scratch,
            compiler_params=params,
        )(local_inverse, values, *margins, basis, lifted, now if last else heat)

    gather_bits = masks()[0]
    *to_send, restricted = surveyed_start()
    sources = gathered(jnp.concatenate([restricted, coarse_inverse], axis=1), gather_bits)
    inverse_rows = sources[:, columns:]
    margins = window_margins(*to_send)
    lifted = summed_shares(inverse_rows, sources[:, :columns], modes)
    now, first, final, left, right = improved(rhs, margins, lifted, None)
    for sweep in range(ITERS - 1):
        around = edges(first, final, "grp") + edges(left, right, "mem")
        residual, *to_send, restricted = surveyed_residual(now, around)
        sources = gathered(restricted, gather_bits)
        margins = window_margins(*to_send)
        lifted = summed_shares(inverse_rows, sources, modes)
        now = improved(residual, margins, lifted, now)[0]
    return now


def solution(mesh):
    placed = (
        P("grp", "mem", None),
        P("grp", "mem"),
        P(("grp", "mem"), None),
        P("grp", "mem", None),
        P(("grp", "mem"), None),
    )
    return jax.shard_map(
        on_device, mesh=mesh, in_specs=placed, out_specs=P("grp", "mem", None), check_vma=False
    )
```

```python
import functools

import jax
import jax.numpy as jnp
from jax import lax
from jax.experimental import pallas as pl
from jax.experimental.pallas import tpu as pltpu
from jax.sharding import PartitionSpec as P

OV = 4
ITERS = 2
LANES = 128
AXES = ("grp", "mem")
EXACT = lax.Precision.HIGHEST
F32 = jnp.float32
BF16 = jnp.bfloat16


def neighbour_pairs(count, first):
    pairs = [(i, i + 1) for i in range(first, count - 1, 2)]
    return pairs + [(j, i) for i, j in pairs]


def edges(low_edge, high_edge, axis):
    count = lax.axis_size(axis)
    even = lax.axis_index(axis) % 2 == 0
    first = lax.ppermute(jnp.where(even, high_edge, low_edge), axis, neighbour_pairs(count, 0))
    second = lax.ppermute(jnp.where(even, low_edge, high_edge), axis, neighbour_pairs(count, 1))
    return jnp.where(even, second, first), jnp.where(even, first, second)


def masks():
    members, groups = lax.axis_size("mem"), lax.axis_size("grp")
    mem_bits = [1 << k for k in range(members.bit_length() - 1)]
    grp_bits = [members << k for k in range(groups.bit_length() - 1)]
    return mem_bits[:0:-1] + grp_bits[:1], mem_bits[:1] + grp_bits[1:]


def swap(value, bit):
    total = lax.axis_size("grp") * lax.axis_size("mem")
    return lax.ppermute(value, AXES, [(i, i ^ bit) for i in range(total)])


def gathered(value, bits):
    for bit in bits:
        value = jnp.concatenate([value, swap(value, bit)], axis=0)
    return value


def summed_shares(inverse_rows, sources, modes):
    shares = lax.dot_general(
        inverse_rows,
        sources,
        (((0,), (0,)), ((), ())),
        precision=EXACT,
        preferred_element_type=F32,
    )
    sum_bits = masks()[1]
    me = lax.axis_index(AXES)
    targets = [0]
    for bit in sum_bits[::-1]:
        targets = targets + [t ^ bit for t in targets]
    parts = [
        lax.dynamic_slice_in_dim(shares, (me ^ target) * modes, modes, 0) for target in targets
    ]
    for bit in sum_bits:
        half = len(parts) // 2
        got = swap(jnp.concatenate(parts[half:], axis=0), bit)
        parts = [part + got[k * modes : (k + 1) * modes] for k, part in enumerate(parts[:half])]
    return parts[0]


def split(values):
    high = values.astype(BF16)
    rest = values - high.astype(F32)
    middle = rest.astype(BF16)
    return high, middle, (rest - middle.astype(F32)).astype(BF16)


def product(a, b):
    return jnp.dot(a, b, preferred_element_type=F32)


def modes_of(basis_ref, first, rows):
    return split(jnp.concatenate([basis_ref[first + k] for k in range(rows)], axis=1))


def restrict(basis_ref, first, block):
    rows, own_y, columns = block.shape
    high, middle, low = modes_of(basis_ref, first, rows)
    modes = high.shape[0]
    block_high, block_middle, block_low = split(block.reshape(rows * own_y, columns))
    three = product(jnp.concatenate([high, middle, low], axis=0), block_high)
    two = product(jnp.concatenate([high, middle], axis=0), block_middle)
    one = product(high, block_low)
    return one + (two[modes:] + three[2 * modes :]) + (two[:modes] + three[modes : 2 * modes]) + three[:modes]


def survey(block, basis_ref, first, low_ref, high_ref, side_ref):
    rows, own_y, columns = block.shape
    if first == 0:
        low_ref[...] = block[:OV].astype(BF16)
    if first + rows == side_ref.shape[0]:
        high_ref[...] = block[rows - OV :].astype(BF16)
    left = lax.broadcasted_iota(jnp.int32, (rows, 2 * OV, columns), 1) < OV
    side_ref[first : first + rows] = jnp.where(
        left, block[:, : 2 * OV], block[:, own_y - 2 * OV :]
    ).astype(BF16)
    return restrict(basis_ref, first, block)


def start_kernel(rhs_ref, basis_ref, low_ref, high_ref, side_ref, sum_ref, held, arrived):
    own_x = held.shape[0]
    copies = [
        pltpu.make_async_copy(
            rhs_ref.at[pl.ds(first, OV)], held.at[pl.ds(first, OV)], arrived.at[first // OV]
        )
        for first in range(0, own_x, OV)
    ]
    for copy in copies:
        copy.start()
    total = jnp.zeros(sum_ref.shape, F32)
    for first in range(0, own_x, OV):
        copies[first // OV].wait()
        block = held[first : first + OV]
        total = total + survey(block, basis_ref, first, low_ref, high_ref, side_ref)
    sum_ref[...] = total


def residual_kernel(
    rhs_ref,
    now_ref,
    below_ref,
    above_ref,
    left_ref,
    right_ref,
    heat_ref,
    basis_ref,
    out_ref,
    low_ref,
    high_ref,
    side_ref,
    sum_ref,
):
    own_x, own_y, columns = now_ref.shape
    place = lax.broadcasted_iota(jnp.int32, (own_y, columns), 0)
    place_heat = place[:, :LANES]

    def flux(values, heat, other, other_heat):
        face = 0.5 * (heat + other_heat)
        return jnp.concatenate([face] * (columns // LANES), axis=1) * (values - other)

    def parts(row):
        return row[:, :columns], row[:, columns:]

    here, heat = now_ref[0], heat_ref[0]
    before = flux(*parts(below_ref[0]), here, heat)
    total = jnp.zeros(sum_ref.shape, F32)
    for index in range(own_x):
        if index + 1 < own_x:
            after, after_heat = now_ref[index + 1], heat_ref[index + 1]
        else:
            after, after_heat = parts(above_ref[0])
        across = flux(here, heat, after, after_heat)
        right, right_heat = parts(right_ref[index // OV, index % OV : index % OV + 1])
        left, left_heat = parts(left_ref[index // OV, index % OV : index % OV + 1])
        right = jnp.where(place == own_y - 1, right, pltpu.roll(here, own_y - 1, 0))
        right_heat = jnp.where(place_heat == own_y - 1, right_heat, pltpu.roll(heat, own_y - 1, 0))
        along = flux(here, heat, right, right_heat)
        entering = jnp.where(
            place == 0, flux(left, left_heat, here[:1], heat[:1]), pltpu.roll(along, 1, 0)
        )
        out_ref[index] = rhs_ref[index] - ((across - before) + (along - entering))
        here, heat, before = after, after_heat, across
        if index % OV == OV - 1:
            first = index + 1 - OV
            block = out_ref[first : first + OV]
            total = total + survey(block, basis_ref, first, low_ref, high_ref, side_ref)
    sum_ref[...] = total


def fine_kernel(
    last,
    inverse_ref,
    block_ref,
    low_ref,
    high_ref,
    side_ref,
    basis_ref,
    lifted_ref,
    extra_ref,
    out_ref,
    *refs,
):
    if last:
        rows_held, window, wide, solved, arrived, result, left_for = refs
    else:
        first_ref, last_ref, left_ref, right_ref, rows_held, window, wide, solved, arrived = refs
        result = out_ref
    own_x, own_y, columns = block_ref.shape
    span_y = own_y + 2 * OV
    rows = solved.shape[0] // span_y
    copies = []
    for first in range(0, own_x, rows):
        count = rows * span_y
        copies.append(
            pltpu.make_async_copy(
                inverse_ref.at[pl.ds((OV + first) * span_y, count)],
                rows_held.at[pl.ds(first * span_y, count)],
                arrived.at[first // rows],
            )
        )
        copies[-1].start()

    def place(index, values):
        wide[OV : OV + own_y, :] = values
        sides = side_ref[index].astype(F32)
        wide[:OV, :] = sides[:OV]
        wide[OV + own_y :, :] = sides[OV:]
        window[index * span_y : (index + 1) * span_y, :] = wide[...].astype(BF16)

    for index in range(OV):
        place(index, low_ref[index].astype(F32))
        place(OV + own_x + index, high_ref[index].astype(F32))
    for index in range(own_x):
        place(OV + index, block_ref[index])

    high, middle, low = split(lifted_ref[...])
    lifted = jnp.concatenate([high, middle, high, low, middle, high], axis=0)
    sends = []
    for first in range(0, own_x, rows):
        copies[first // rows].wait()
        solved[...] = product(
            rows_held[first * span_y : (first + rows) * span_y, :], window[...]
        )
        high, middle, low = modes_of(basis_ref, first, rows)
        coarse = lax.dot_general(
            jnp.concatenate([high, high, middle, high, middle, low], axis=0),
            lifted,
            (((0,), (0,)), ((), ())),
            preferred_element_type=F32,
        )
        for k in range(rows):
            value = solved[k * span_y + OV : k * span_y + OV + own_y, :]
            value = value + coarse[k * own_y : (k + 1) * own_y]
            if last:
                value = extra_ref[first + k] + value
            result[first + k] = value
        if last:
            sends.append(
                pltpu.make_async_copy(
                    result.at[pl.ds(first, rows)],
                    out_ref.at[pl.ds(first, rows)],
                    left_for.at[first // rows],
                )
            )
            sends[-1].start()
        else:
            for index in range(first, first + rows):
                for ref, at in ((left_ref, 0), (right_ref, own_y - 1)):
                    row = pl.ds(index % OV, 1)
                    ref[index // OV, row, :columns] = result[index, at : at + 1]
                    ref[index // OV, row, columns:] = extra_ref[index, at : at + 1]
    for send in sends:
        send.wait()
    if not last:
        first_ref[0] = jnp.concatenate([result[0], extra_ref[0]], axis=1)
        last_ref[0] = jnp.concatenate([result[own_x - 1], extra_ref[own_x - 1]], axis=1)


def shape_of(shape, kind):
    return jax.ShapeDtypeStruct(shape, kind)


def on_device(rhs, conductivity, local_inverse, coarse_basis, coarse_inverse):
    own_x, own_y, columns = rhs.shape
    modes = coarse_basis.shape[2]
    span_x = own_x + 2 * OV
    span_y = own_y + 2 * OV
    local = span_x * span_y
    basis = jnp.transpose(coarse_basis, (0, 2, 1))
    heat = jnp.broadcast_to(conductivity[:, :, None], (own_x, own_y, LANES))

    def params(mebibytes):
        return pltpu.CompilerParams(vmem_limit_bytes=mebibytes * 2**20)

    group = 2 * OV if own_x % (2 * OV) == 0 else OV
    in_vmem = pl.BlockSpec(memory_space=pltpu.VMEM)
    in_hbm = pl.BlockSpec(memory_space=pltpu.HBM)

    survey_shapes = [
        shape_of((OV, own_y, columns), BF16),
        shape_of((OV, own_y, columns), BF16),
        shape_of((own_x, 2 * OV, columns), BF16),
        shape_of((modes, columns), F32),
    ]

    def surveyed_start():
        return pl.pallas_call(
            start_kernel,
            in_specs=[in_hbm, in_vmem],
            out_specs=[in_vmem] * 4,
            out_shape=survey_shapes,
            scratch_shapes=[
                pltpu.VMEM(rhs.shape, F32),
                pltpu.SemaphoreType.DMA((own_x // OV,)),
            ],
            compiler_params=params(8),
        )(pltpu.with_memory_space_constraint(rhs, pltpu.HBM), basis)

    def surveyed_residual(now, around):
        return pl.pallas_call(
            residual_kernel,
            in_specs=[in_vmem] * 8,
            out_specs=[in_vmem] * 5,
            out_shape=[shape_of(rhs.shape, F32)] + survey_shapes,
            compiler_params=params(16),
        )(rhs, now, *around, heat, basis)

    def window_margins(low_edge, high_edge, sides):
        low, high = edges(low_edge, high_edge, "grp")
        corners = [jnp.concatenate([m[:, :OV], m[:, -OV:]], axis=1) for m in (low, high)]
        sides = jnp.concatenate([corners[0], sides, corners[1]], axis=0)
        left, right = edges(sides[:, :OV], sides[:, OV:], "mem")
        return low, high, jnp.concatenate([left, right], axis=1)

    def improved(values, margins, lifted, now):
        last = now is not None
        edge = columns + LANES
        out_shape = [shape_of(rhs.shape, F32)]
        scratch = [
            pltpu.VMEM((own_x * span_y, local), BF16),
            pltpu.VMEM((local, columns), BF16),
            pltpu.VMEM((span_y, columns), F32),
            pltpu.VMEM((group * span_y, columns), F32),
            pltpu.SemaphoreType.DMA((own_x // group,)),
        ]
        if last:
            out_specs = [in_hbm]
            scratch += [pltpu.VMEM(rhs.shape, F32), pltpu.SemaphoreType.DMA((own_x // group,))]
        else:
            out_specs = [in_vmem] * 5
            out_shape += [shape_of((1, own_y, edge), F32)] * 2
            out_shape += [shape_of((own_x // OV, OV, edge), F32)] * 2
        return pl.pallas_call(
            functools.partial(fine_kernel, last),
            in_specs=[in_hbm] + [in_vmem] * 7,
            out_specs=out_specs,
            out_shape=out_shape,
            scratch_shapes=scratch,
            compiler_params=params(24),
        )(
            pltpu.with_memory_space_constraint(local_inverse, pltpu.HBM),
            values,
            *margins,
            basis,
            lifted,
            now if last else heat,
        )

    gather_bits = masks()[0]
    *to_send, restricted = surveyed_start()
    sources = gathered(jnp.concatenate([restricted, coarse_inverse], axis=1), gather_bits)
    inverse_rows = sources[:, columns:]
    margins = window_margins(*to_send)
    lifted = summed_shares(inverse_rows, sources[:, :columns], modes)
    now, first, final, left, right = improved(rhs, margins, lifted, None)
    for sweep in range(ITERS - 1):
        around = edges(first, final, "grp") + edges(left, right, "mem")
        residual, *to_send, restricted = surveyed_residual(now, around)
        sources = gathered(restricted, gather_bits)
        margins = window_margins(*to_send)
        lifted = summed_shares(inverse_rows, sources, modes)
        now = improved(residual, margins, lifted, now)[0]
    return now


def solution(mesh):
    placed = (
        P("grp", "mem", None),
        P("grp", "mem"),
        P(("grp", "mem"), None),
        P("grp", "mem", None),
        P(("grp", "mem"), None),
    )
    return jax.shard_map(
        on_device, mesh=mesh, in_specs=placed, out_specs=P("grp", "mem", None), check_vma=False
    )
```

```python
import functools

import jax
import jax.numpy as jnp
from jax import lax
from jax.experimental import pallas as pl
from jax.experimental.pallas import tpu as pltpu
from jax.sharding import PartitionSpec as P

OV = 4
ITERS = 2
AHEAD = 2
LANES = 128
AXES = ("grp", "mem")
EXACT = lax.Precision.HIGHEST
F32 = jnp.float32
BF16 = jnp.bfloat16


def edges(low_edge, high_edge, axis):
    count = lax.axis_size(axis)
    index = lax.axis_index(axis)
    up = [(i, (i + 1) % count) for i in range(count)]
    low = lax.ppermute(high_edge, axis, up)
    high = lax.ppermute(low_edge, axis, [(j, i) for i, j in up])
    return jnp.where(index == 0, 0, low), jnp.where(index == count - 1, 0, high)


def masks():
    members, groups = lax.axis_size("mem"), lax.axis_size("grp")
    mem_bits = [1 << k for k in range(members.bit_length() - 1)]
    grp_bits = [members << k for k in range(groups.bit_length() - 1)]
    return mem_bits[:0:-1] + grp_bits[:1], mem_bits[:1] + grp_bits[1:]


def swap(value, bit):
    total = lax.axis_size("grp") * lax.axis_size("mem")
    return lax.ppermute(value, AXES, [(i, i ^ bit) for i in range(total)])


def gathered(value, bits):
    for bit in bits:
        value = jnp.concatenate([value, swap(value, bit)], axis=0)
    return value


def summed_shares(inverse_rows, sources, modes):
    shares = lax.dot_general(
        inverse_rows,
        sources,
        (((0,), (0,)), ((), ())),
        precision=EXACT,
        preferred_element_type=F32,
    )
    sum_bits = masks()[1]
    me = lax.axis_index(AXES)
    targets = [0]
    for bit in sum_bits[::-1]:
        targets = targets + [t ^ bit for t in targets]
    parts = [
        lax.dynamic_slice_in_dim(shares, (me ^ target) * modes, modes, 0) for target in targets
    ]
    for bit in sum_bits:
        half = len(parts) // 2
        got = swap(jnp.concatenate(parts[half:], axis=0), bit)
        parts = [part + got[k * modes : (k + 1) * modes] for k, part in enumerate(parts[:half])]
    return parts[0]


def split(values):
    high = values.astype(BF16)
    rest = values - high.astype(F32)
    middle = rest.astype(BF16)
    return high, middle, (rest - middle.astype(F32)).astype(BF16)


def product(a, b):
    return jnp.dot(a, b, preferred_element_type=F32)


def modes_of(basis_ref, first, rows):
    return split(jnp.concatenate([basis_ref[first + k] for k in range(rows)], axis=1))


def restrict(basis_ref, first, block):
    rows, own_y, columns = block.shape
    high, middle, low = modes_of(basis_ref, first, rows)
    modes = high.shape[0]
    block_high, block_middle, block_low = split(block.reshape(rows * own_y, columns))
    three = product(jnp.concatenate([high, middle, low], axis=0), block_high)
    two = product(jnp.concatenate([high, middle], axis=0), block_middle)
    one = product(high, block_low)
    return one + (two[modes:] + three[2 * modes :]) + (two[:modes] + three[modes : 2 * modes]) + three[:modes]


def survey(block, basis_ref, first, low_ref, high_ref, side_ref):
    rows, own_y, columns = block.shape
    if first == 0:
        low_ref[...] = block[:OV].astype(BF16)
    if first + rows == side_ref.shape[0]:
        high_ref[...] = block[rows - OV :].astype(BF16)
    left = lax.broadcasted_iota(jnp.int32, (rows, 2 * OV, columns), 1) < OV
    side_ref[first : first + rows] = jnp.where(
        left, block[:, : 2 * OV], block[:, own_y - 2 * OV :]
    ).astype(BF16)
    return restrict(basis_ref, first, block)


def start_kernel(rhs_ref, basis_ref, low_ref, high_ref, side_ref, sum_ref, held, arrived):
    own_x = held.shape[0]
    copies = [
        pltpu.make_async_copy(
            rhs_ref.at[pl.ds(first, OV)], held.at[pl.ds(first, OV)], arrived.at[first // OV]
        )
        for first in range(0, own_x, OV)
    ]
    for copy in copies:
        copy.start()
    total = jnp.zeros(sum_ref.shape, F32)
    for first in range(0, own_x, OV):
        copies[first // OV].wait()
        block = held[first : first + OV]
        total = total + survey(block, basis_ref, first, low_ref, high_ref, side_ref)
    sum_ref[...] = total


def residual_kernel(
    rhs_ref,
    now_ref,
    below_ref,
    above_ref,
    left_ref,
    right_ref,
    heat_ref,
    basis_ref,
    out_ref,
    low_ref,
    high_ref,
    side_ref,
    sum_ref,
):
    own_x, own_y, columns = now_ref.shape
    place = lax.broadcasted_iota(jnp.int32, (own_y, columns), 0)
    place_heat = place[:, :LANES]

    def flux(values, heat, other, other_heat):
        face = 0.5 * (heat + other_heat)
        return jnp.concatenate([face] * (columns // LANES), axis=1) * (values - other)

    def parts(row):
        return row[:, :columns], row[:, columns:]

    here, heat = now_ref[0], heat_ref[0]
    before = flux(*parts(below_ref[0]), here, heat)
    total = jnp.zeros(sum_ref.shape, F32)
    for index in range(own_x):
        if index + 1 < own_x:
            after, after_heat = now_ref[index + 1], heat_ref[index + 1]
        else:
            after, after_heat = parts(above_ref[0])
        across = flux(here, heat, after, after_heat)
        right, right_heat = parts(right_ref[index // OV, index % OV : index % OV + 1])
        left, left_heat = parts(left_ref[index // OV, index % OV : index % OV + 1])
        right = jnp.where(place == own_y - 1, right, pltpu.roll(here, own_y - 1, 0))
        right_heat = jnp.where(place_heat == own_y - 1, right_heat, pltpu.roll(heat, own_y - 1, 0))
        along = flux(here, heat, right, right_heat)
        entering = jnp.where(
            place == 0, flux(left, left_heat, here[:1], heat[:1]), pltpu.roll(along, 1, 0)
        )
        out_ref[index] = rhs_ref[index] - ((across - before) + (along - entering))
        here, heat, before = after, after_heat, across
        if index % OV == OV - 1:
            first = index + 1 - OV
            block = out_ref[first : first + OV]
            total = total + survey(block, basis_ref, first, low_ref, high_ref, side_ref)
    sum_ref[...] = total


def fine_kernel(fetch, inverse_ref, block_ref, low_ref, high_ref, side_ref, out_ref, *refs):
    own_x, own_y, columns = block_ref.shape
    span_y = own_y + 2 * OV
    copies = []
    if fetch:
        rows_held, window, wide, solved, arrived = refs
        rows = solved.shape[0] // span_y
        for first in range(0, own_x, rows):
            count = rows * span_y
            copies.append(
                pltpu.make_async_copy(
                    inverse_ref.at[pl.ds((OV + first) * span_y, count)],
                    rows_held.at[pl.ds(first * span_y, count)],
                    arrived.at[first // rows],
                )
            )
        for copy in copies[:AHEAD]:
            copy.start()
    else:
        rows_held = inverse_ref
        window, wide, solved = refs
        rows = solved.shape[0] // span_y

    def place(index, values):
        wide[OV : OV + own_y, :] = values
        sides = side_ref[index].astype(F32)
        wide[:OV, :] = sides[:OV]
        wide[OV + own_y :, :] = sides[OV:]
        window[index * span_y : (index + 1) * span_y, :] = wide[...].astype(BF16)

    for index in range(OV):
        place(index, low_ref[index].astype(F32))
        place(OV + own_x + index, high_ref[index].astype(F32))
    for index in range(own_x):
        place(OV + index, block_ref[index])

    for first in range(0, own_x, rows):
        if fetch:
            copies[first // rows].wait()
            for copy in copies[first // rows + AHEAD : first // rows + AHEAD + 1]:
                copy.start()
        solved[...] = product(
            rows_held[first * span_y : (first + rows) * span_y, :], window[...]
        )
        for k in range(rows):
            out_ref[first + k] = solved[k * span_y + OV : k * span_y + OV + own_y, :]


def update_kernel(last, fine_ref, basis_ref, lifted_ref, extra_ref, out_ref, *refs):
    own_x, own_y, columns = fine_ref.shape
    if last:
        result, left_for = refs
    else:
        first_ref, last_ref, left_ref, right_ref = refs
        result = out_ref
    high, middle, low = split(lifted_ref[...])
    lifted = jnp.concatenate([high, middle, high, low, middle, high], axis=0)
    sends = []
    for first in range(0, own_x, OV):
        high, middle, low = modes_of(basis_ref, first, OV)
        coarse = lax.dot_general(
            jnp.concatenate([high, high, middle, high, middle, low], axis=0),
            lifted,
            (((0,), (0,)), ((), ())),
            preferred_element_type=F32,
        )
        for k in range(OV):
            value = fine_ref[first + k] + coarse[k * own_y : (k + 1) * own_y]
            if last:
                value = extra_ref[first + k] + value
            result[first + k] = value
        if last:
            sends.append(
                pltpu.make_async_copy(
                    result.at[pl.ds(first, OV)],
                    out_ref.at[pl.ds(first, OV)],
                    left_for.at[first // OV],
                )
            )
            sends[-1].start()
        else:
            for k in range(OV):
                for ref, at in ((left_ref, 0), (right_ref, own_y - 1)):
                    ref[first // OV, k : k + 1, :columns] = result[first + k, at : at + 1]
                    ref[first // OV, k : k + 1, columns:] = extra_ref[first + k, at : at + 1]
    for send in sends:
        send.wait()
    if not last:
        first_ref[0] = jnp.concatenate([result[0], extra_ref[0]], axis=1)
        last_ref[0] = jnp.concatenate([result[own_x - 1], extra_ref[own_x - 1]], axis=1)


def shape_of(shape, kind):
    return jax.ShapeDtypeStruct(shape, kind)


def on_device(rhs, conductivity, local_inverse, coarse_basis, coarse_inverse):
    own_x, own_y, columns = rhs.shape
    modes = coarse_basis.shape[2]
    span_x = own_x + 2 * OV
    span_y = own_y + 2 * OV
    local = span_x * span_y
    basis = jnp.transpose(coarse_basis, (0, 2, 1))
    heat = jnp.broadcast_to(conductivity[:, :, None], (own_x, own_y, LANES))

    def params(mebibytes):
        return pltpu.CompilerParams(vmem_limit_bytes=mebibytes * 2**20)

    group = 2 * OV if own_x % (2 * OV) == 0 else OV
    in_vmem = pl.BlockSpec(memory_space=pltpu.VMEM)
    in_hbm = pl.BlockSpec(memory_space=pltpu.HBM)

    survey_shapes = [
        shape_of((OV, own_y, columns), BF16),
        shape_of((OV, own_y, columns), BF16),
        shape_of((own_x, 2 * OV, columns), BF16),
        shape_of((modes, columns), F32),
    ]

    def surveyed_start():
        return pl.pallas_call(
            start_kernel,
            in_specs=[in_hbm, in_vmem],
            out_specs=[in_vmem] * 4,
            out_shape=survey_shapes,
            scratch_shapes=[
                pltpu.VMEM(rhs.shape, F32),
                pltpu.SemaphoreType.DMA((own_x // OV,)),
            ],
            compiler_params=params(8),
        )(pltpu.with_memory_space_constraint(rhs, pltpu.HBM), basis)

    def surveyed_residual(now, around):
        return pl.pallas_call(
            residual_kernel,
            in_specs=[in_vmem] * 8,
            out_specs=[in_vmem] * 5,
            out_shape=[shape_of(rhs.shape, F32)] + survey_shapes,
            compiler_params=params(16),
        )(rhs, now, *around, heat, basis)

    def window_margins(low_edge, high_edge, sides):
        low, high = edges(low_edge, high_edge, "grp")
        corners = [jnp.concatenate([m[:, :OV], m[:, -OV:]], axis=1) for m in (low, high)]
        sides = jnp.concatenate([corners[0], sides, corners[1]], axis=0)
        left, right = edges(sides[:, :OV], sides[:, OV:], "mem")
        return low, high, jnp.concatenate([left, right], axis=1)

    held = (own_x * span_y, local)

    def fine(rows, values, margins):
        fetch = rows.shape != held
        out_shape = [shape_of(rhs.shape, F32)]
        scratch = [
            pltpu.VMEM((local, columns), BF16),
            pltpu.VMEM((span_y, columns), F32),
            pltpu.VMEM((group * span_y, columns), F32),
        ]
        if fetch:
            rows = pltpu.with_memory_space_constraint(rows, pltpu.HBM)
            out_shape.append(shape_of(held, BF16))
            scratch.append(pltpu.SemaphoreType.DMA((own_x // group,)))
        result = pl.pallas_call(
            functools.partial(fine_kernel, fetch),
            in_specs=[in_hbm if fetch else in_vmem] + [in_vmem] * 4,
            out_specs=[in_vmem] * len(out_shape),
            out_shape=out_shape,
            scratch_shapes=scratch,
            compiler_params=params(24),
            cost_estimate=pl.CostEstimate(
                flops=2 * held[0] * local * columns,
                bytes_accessed=2 * held[0] * local,
                transcendentals=0,
            ),
        )(rows, values, *margins)
        return result if fetch else (*result, rows)

    def updated(solved, lifted, now):
        last = now is not None
        edge = columns + LANES
        out_shape = [shape_of(rhs.shape, F32)]
        if last:
            out_specs = [in_hbm]
            scratch = [pltpu.VMEM(rhs.shape, F32), pltpu.SemaphoreType.DMA((own_x // OV,))]
        else:
            out_specs = [in_vmem] * 5
            out_shape += [shape_of((1, own_y, edge), F32)] * 2
            out_shape += [shape_of((own_x // OV, OV, edge), F32)] * 2
            scratch = []
        return pl.pallas_call(
            functools.partial(update_kernel, last),
            in_specs=[in_vmem] * 4,
            out_specs=out_specs,
            out_shape=out_shape,
            scratch_shapes=scratch,
            compiler_params=params(16),
        )(solved, basis, lifted, now if last else heat)

    gather_bits = masks()[0]
    *to_send, restricted = surveyed_start()
    sources = gathered(jnp.concatenate([restricted, coarse_inverse], axis=1), gather_bits)
    inverse_rows = sources[:, columns:]
    margins = window_margins(*to_send)
    solved, rows = fine(local_inverse, rhs, margins)
    lifted = summed_shares(inverse_rows, sources[:, :columns], modes)
    now, first, final, left, right = updated(solved, lifted, None)
    for sweep in range(ITERS - 1):
        around = edges(first, final, "grp") + edges(left, right, "mem")
        residual, *to_send, restricted = surveyed_residual(now, around)
        sources = gathered(restricted, gather_bits)
        margins = window_margins(*to_send)
        solved, rows = fine(rows, residual, margins)
        lifted = summed_shares(inverse_rows, sources, modes)
        now = updated(solved, lifted, now)[0]
    return now


def solution(mesh):
    placed = (
        P("grp", "mem", None),
        P("grp", "mem"),
        P(("grp", "mem"), None),
        P("grp", "mem", None),
        P(("grp", "mem"), None),
    )
    return jax.shard_map(
        on_device, mesh=mesh, in_specs=placed, out_specs=P("grp", "mem", None), check_vma=False
    )
```

```python
import functools

import jax
import jax.numpy as jnp
from jax import lax
from jax.experimental import pallas as pl
from jax.experimental.pallas import tpu as pltpu
from jax.sharding import PartitionSpec as P

OV = 4
ITERS = 2
AHEAD = 2
ORDER = range
LANES = 128
EXACT = lax.Precision.HIGHEST
F32 = jnp.float32
BF16 = jnp.bfloat16


def shifted(value, axis, distance):
    count = lax.axis_size(axis)
    return lax.ppermute(value, axis, [(i, (i + distance) % count) for i in range(count)])


def edges(low_edge, high_edge, axis):
    return beyond(shifted(high_edge, axis, 1), shifted(low_edge, axis, -1), axis)


def beyond(low, high, axis):
    index = lax.axis_index(axis)
    last = lax.axis_size(axis) - 1
    return jnp.where(index == 0, 0, low), jnp.where(index == last, 0, high)


def summed_over_members(shares):
    members = lax.axis_size("mem")
    sizes = [2] * (members.bit_length() - 1)
    shares = shares.reshape(*sizes, shares.shape[0] // members, shares.shape[1])
    for k in ORDER(len(sizes)):
        bit = lax.axis_index("mem") >> k & 1
        axis = len(sizes) - 1 - k
        keep = lax.dynamic_slice_in_dim(shares, bit, 1, axis)
        send = lax.dynamic_slice_in_dim(shares, 1 - bit, 1, axis)
        pairs = [(i, i ^ 1 << k) for i in range(members)]
        shares = keep + lax.ppermute(send, "mem", pairs)
    return shares.reshape(shares.shape[-2:])


def split(values):
    high = values.astype(BF16)
    rest = values - high.astype(F32)
    middle = rest.astype(BF16)
    return high, middle, (rest - middle.astype(F32)).astype(BF16)


def product(a, b):
    return jnp.dot(a, b, preferred_element_type=F32)


def modes_of(basis_ref, first, rows):
    return split(jnp.concatenate([basis_ref[first + k] for k in range(rows)], axis=1))


def restrict(basis_ref, first, block):
    rows, own_y, columns = block.shape
    high, middle, low = modes_of(basis_ref, first, rows)
    modes = high.shape[0]
    block_high, block_middle, block_low = split(block.reshape(rows * own_y, columns))
    three = product(jnp.concatenate([high, middle, low], axis=0), block_high)
    two = product(jnp.concatenate([high, middle], axis=0), block_middle)
    one = product(high, block_low)
    return one + (two[modes:] + three[2 * modes :]) + (two[:modes] + three[modes : 2 * modes]) + three[:modes]


def survey(block, basis_ref, first, down_ref, up_ref, side_ref):
    rows, own_y, columns = block.shape
    count = OV * own_y
    if first == 0:
        down_ref[:count] = block[:OV].reshape(count, columns).astype(BF16)
    if first + rows == side_ref.shape[0]:
        up_ref[:count] = block[rows - OV :].reshape(count, columns).astype(BF16)
    left = lax.broadcasted_iota(jnp.int32, (rows, 2 * OV, columns), 1) < OV
    side_ref[first : first + rows] = jnp.where(
        left, block[:, : 2 * OV], block[:, own_y - 2 * OV :]
    ).astype(BF16)
    return restrict(basis_ref, first, block)


def finish(total, start, down_ref, up_ref, sum_ref):
    sum_ref[...] = total
    parts = jnp.concatenate(split(total), axis=0)
    end = start + parts.shape[0]
    down_ref[start:end] = parts
    up_ref[start:end] = parts
    return end


def start_kernel(
    rhs_ref, basis_ref, inverse_ref, down_ref, up_ref, side_ref, sum_ref, held, arrived
):
    own_x, own_y, columns = held.shape
    copies = [
        pltpu.make_async_copy(
            rhs_ref.at[pl.ds(first, OV)], held.at[pl.ds(first, OV)], arrived.at[first // OV]
        )
        for first in range(0, own_x, OV)
    ]
    for copy in copies:
        copy.start()

    groups = lax.axis_size("grp")
    width = inverse_ref.shape[1] // groups
    modes = inverse_ref.shape[0]
    start = OV * own_y + 3 * modes
    for ref, step in ((up_ref, 1), (down_ref, groups - 1)):
        group = lax.rem(lax.axis_index("grp") + step, groups)
        wanted = inverse_ref[:, pl.ds(pl.multiple_of(group * width, width), width)]
        parts = jnp.concatenate(split(wanted), axis=1)
        for k in range(3 * width // columns):
            ref[start + k * modes : start + (k + 1) * modes] = parts[
                :, k * columns : (k + 1) * columns
            ]

    total = jnp.zeros(sum_ref.shape, F32)
    for first in range(0, own_x, OV):
        copies[first // OV].wait()
        block = held[first : first + OV]
        total = total + survey(block, basis_ref, first, down_ref, up_ref, side_ref)
    finish(total, OV * own_y, down_ref, up_ref, sum_ref)


def residual_kernel(
    rhs_ref,
    now_ref,
    below_ref,
    above_ref,
    left_ref,
    right_ref,
    heat_ref,
    basis_ref,
    out_ref,
    down_ref,
    up_ref,
    side_ref,
    sum_ref,
):
    own_x, own_y, columns = now_ref.shape
    place = lax.broadcasted_iota(jnp.int32, (own_y, columns), 0)
    place_heat = place[:, :LANES]

    def flux(values, heat, other, other_heat):
        face = 0.5 * (heat + other_heat)
        return jnp.concatenate([face] * (columns // LANES), axis=1) * (values - other)

    def parts(row):
        return row[:, :columns], row[:, columns:]

    here, heat = now_ref[0], heat_ref[0]
    before = flux(*parts(below_ref[0]), here, heat)
    total = jnp.zeros(sum_ref.shape, F32)
    for index in range(own_x):
        if index + 1 < own_x:
            after, after_heat = now_ref[index + 1], heat_ref[index + 1]
        else:
            after, after_heat = parts(above_ref[0])
        across = flux(here, heat, after, after_heat)
        right, right_heat = parts(right_ref[index // OV, index % OV : index % OV + 1])
        left, left_heat = parts(left_ref[index // OV, index % OV : index % OV + 1])
        right = jnp.where(place == own_y - 1, right, pltpu.roll(here, own_y - 1, 0))
        right_heat = jnp.where(place_heat == own_y - 1, right_heat, pltpu.roll(heat, own_y - 1, 0))
        along = flux(here, heat, right, right_heat)
        entering = jnp.where(
            place == 0, flux(left, left_heat, here[:1], heat[:1]), pltpu.roll(along, 1, 0)
        )
        out_ref[index] = rhs_ref[index] - ((across - before) + (along - entering))
        here, heat, before = after, after_heat, across
        if index % OV == OV - 1:
            first = index + 1 - OV
            block = out_ref[first : first + OV]
            total = total + survey(block, basis_ref, first, down_ref, up_ref, side_ref)
    finish(total, OV * own_y, down_ref, up_ref, sum_ref)


def fine_kernel(fetch, inverse_ref, block_ref, low_ref, high_ref, side_ref, out_ref, *refs):
    own_x, own_y, columns = block_ref.shape
    span_y = own_y + 2 * OV
    copies = []
    if fetch:
        rows_held, window, wide, solved, arrived = refs
        rows = solved.shape[0] // span_y
        for first in range(0, own_x, rows):
            count = rows * span_y
            copies.append(
                pltpu.make_async_copy(
                    inverse_ref.at[pl.ds((OV + first) * span_y, count)],
                    rows_held.at[pl.ds(first * span_y, count)],
                    arrived.at[first // rows],
                )
            )
        for copy in copies[:AHEAD]:
            copy.start()
    else:
        rows_held = inverse_ref
        window, wide, solved = refs
        rows = solved.shape[0] // span_y

    def place(index, values):
        wide[OV : OV + own_y, :] = values
        sides = side_ref[index].astype(F32)
        wide[:OV, :] = sides[:OV]
        wide[OV + own_y :, :] = sides[OV:]
        window[index * span_y : (index + 1) * span_y, :] = wide[...].astype(BF16)

    for index in range(OV):
        place(index, low_ref[index].astype(F32))
        place(OV + own_x + index, high_ref[index].astype(F32))
    for index in range(own_x):
        place(OV + index, block_ref[index])

    for first in range(0, own_x, rows):
        if fetch:
            copies[first // rows].wait()
            for copy in copies[first // rows + AHEAD : first // rows + AHEAD + 1]:
                copy.start()
        solved[...] = product(
            rows_held[first * span_y : (first + rows) * span_y, :], window[...]
        )
        for k in range(rows):
            out_ref[first + k] = solved[k * span_y + OV : k * span_y + OV + own_y, :]


def update_kernel(last, fine_ref, basis_ref, lifted_ref, extra_ref, out_ref, *refs):
    own_x, own_y, columns = fine_ref.shape
    if last:
        result, left_for = refs
    else:
        first_ref, last_ref, left_ref, right_ref = refs
        result = out_ref
    high, middle, low = split(lifted_ref[...])
    lifted = jnp.concatenate([high, middle, high, low, middle, high], axis=0)
    sends = []
    for first in range(0, own_x, OV):
        high, middle, low = modes_of(basis_ref, first, OV)
        coarse = lax.dot_general(
            jnp.concatenate([high, high, middle, high, middle, low], axis=0),
            lifted,
            (((0,), (0,)), ((), ())),
            preferred_element_type=F32,
        )
        for k in range(OV):
            value = fine_ref[first + k] + coarse[k * own_y : (k + 1) * own_y]
            if last:
                value = extra_ref[first + k] + value
            result[first + k] = value
        if last:
            sends.append(
                pltpu.make_async_copy(
                    result.at[pl.ds(first, OV)],
                    out_ref.at[pl.ds(first, OV)],
                    left_for.at[first // OV],
                )
            )
            sends[-1].start()
        else:
            for k in range(OV):
                for ref, at in ((left_ref, 0), (right_ref, own_y - 1)):
                    ref[first // OV, k : k + 1, :columns] = result[first + k, at : at + 1]
                    ref[first // OV, k : k + 1, columns:] = extra_ref[first + k, at : at + 1]
    for send in sends:
        send.wait()
    if not last:
        first_ref[0] = jnp.concatenate([result[0], extra_ref[0]], axis=1)
        last_ref[0] = jnp.concatenate([result[own_x - 1], extra_ref[own_x - 1]], axis=1)


def shape_of(shape, kind):
    return jax.ShapeDtypeStruct(shape, kind)


def on_device(rhs, conductivity, local_inverse, coarse_basis, coarse_inverse):
    own_x, own_y, columns = rhs.shape
    modes = coarse_basis.shape[2]
    span_x = own_x + 2 * OV
    span_y = own_y + 2 * OV
    local = span_x * span_y
    basis = jnp.transpose(coarse_basis, (0, 2, 1))
    heat = jnp.broadcast_to(conductivity[:, :, None], (own_x, own_y, LANES))

    def params(mebibytes):
        return pltpu.CompilerParams(vmem_limit_bytes=mebibytes * 2**20)

    group = 2 * OV if own_x % (2 * OV) == 0 else OV
    in_vmem = pl.BlockSpec(memory_space=pltpu.VMEM)
    in_hbm = pl.BlockSpec(memory_space=pltpu.HBM)

    members, groups = lax.axis_size("mem"), lax.axis_size("grp")
    width = members * modes
    edge_rows = OV * own_y
    sum_rows = 3 * modes
    inverse_rows = 3 * width // columns * modes

    def survey_shapes(rows):
        return [
            shape_of((rows, columns), BF16),
            shape_of((rows, columns), BF16),
            shape_of((own_x, 2 * OV, columns), BF16),
            shape_of((modes, columns), F32),
        ]

    def surveyed_start():
        return pl.pallas_call(
            start_kernel,
            in_specs=[in_hbm, in_vmem, in_vmem],
            out_specs=[in_vmem] * 4,
            out_shape=survey_shapes(edge_rows + sum_rows + inverse_rows),
            scratch_shapes=[
                pltpu.VMEM(rhs.shape, F32),
                pltpu.SemaphoreType.DMA((own_x // OV,)),
            ],
            compiler_params=params(8),
        )(pltpu.with_memory_space_constraint(rhs, pltpu.HBM), basis, coarse_inverse)

    def surveyed_residual(now, around):
        return pl.pallas_call(
            residual_kernel,
            in_specs=[in_vmem] * 8,
            out_specs=[in_vmem] * 5,
            out_shape=[shape_of(rhs.shape, F32)] + survey_shapes(edge_rows + sum_rows),
            compiler_params=params(16),
        )(rhs, now, *around, heat, basis)

    def added(parts):
        high, middle, low = (part.astype(F32) for part in parts)
        return high + middle + low

    def sums_in(message):
        return added(jnp.split(message[edge_rows : edge_rows + sum_rows], 3, axis=0))

    def inverse_in(message):
        pieces = message[edge_rows + sum_rows :]
        pieces = jnp.concatenate(jnp.split(pieces, inverse_rows // modes, axis=0), axis=1)
        return added(jnp.split(pieces, 3, axis=1))

    def inverse_for(distance):
        group = (lax.axis_index("grp") + distance) % groups
        return lax.dynamic_slice_in_dim(coarse_inverse, group * width, width, 1)

    def exchanged(down, up, sides, restricted, inverse):
        first = inverse is None
        from_below, from_above = shifted(up, "grp", 1), shifted(down, "grp", -1)
        sums = [restricted]
        rows = [inverse_for(0)]
        for distance in range(2, groups - 1):
            if first:
                message = jnp.concatenate([restricted, inverse_for(distance)], axis=1)
            else:
                message = restricted
            message = shifted(message, "grp", distance)
            sums.append(message[:, :columns])
            rows.append(message[:, columns:])
        for message in (from_below, from_above):
            sums.append(sums_in(message))
            if first:
                rows.append(inverse_in(message))
        if first:
            inverse = jnp.concatenate(rows, axis=0)
        low, high = beyond(from_below[:edge_rows], from_above[:edge_rows], "grp")
        low = low.reshape(OV, own_y, columns)
        high = high.reshape(OV, own_y, columns)
        corners = [jnp.concatenate([m[:, :OV], m[:, -OV:]], axis=1) for m in (low, high)]
        sides = jnp.concatenate([corners[0], sides, corners[1]], axis=0)
        left, right = edges(sides[:, :OV], sides[:, OV:], "mem")
        margins = low, high, jnp.concatenate([left, right], axis=1)
        return margins, jnp.concatenate(sums, axis=0), inverse

    def coarse_solve(inverse, sums):
        shares = lax.dot_general(
            inverse,
            sums,
            (((0,), (0,)), ((), ())),
            precision=EXACT,
            preferred_element_type=F32,
        )
        return summed_over_members(shares)

    held = (own_x * span_y, local)

    def fine(rows, values, margins):
        fetch = rows.shape != held
        out_shape = [shape_of(rhs.shape, F32)]
        scratch = [
            pltpu.VMEM((local, columns), BF16),
            pltpu.VMEM((span_y, columns), F32),
            pltpu.VMEM((group * span_y, columns), F32),
        ]
        if fetch:
            rows = pltpu.with_memory_space_constraint(rows, pltpu.HBM)
            out_shape.append(shape_of(held, BF16))
            scratch.append(pltpu.SemaphoreType.DMA((own_x // group,)))
        result = pl.pallas_call(
            functools.partial(fine_kernel, fetch),
            in_specs=[in_hbm if fetch else in_vmem] + [in_vmem] * 4,
            out_specs=[in_vmem] * len(out_shape),
            out_shape=out_shape,
            scratch_shapes=scratch,
            compiler_params=params(24),
            cost_estimate=pl.CostEstimate(
                flops=2 * held[0] * local * columns,
                bytes_accessed=2 * held[0] * local,
                transcendentals=0,
            ),
        )(rows, values, *margins)
        return result if fetch else (*result, rows)

    def updated(solved, lifted, now):
        last = now is not None
        edge = columns + LANES
        out_shape = [shape_of(rhs.shape, F32)]
        if last:
            out_specs = [in_hbm]
            scratch = [pltpu.VMEM(rhs.shape, F32), pltpu.SemaphoreType.DMA((own_x // OV,))]
        else:
            out_specs = [in_vmem] * 5
            out_shape += [shape_of((1, own_y, edge), F32)] * 2
            out_shape += [shape_of((own_x // OV, OV, edge), F32)] * 2
            scratch = []
        return pl.pallas_call(
            functools.partial(update_kernel, last),
            in_specs=[in_vmem] * 4,
            out_specs=out_specs,
            out_shape=out_shape,
            scratch_shapes=scratch,
            compiler_params=params(16),
        )(solved, basis, lifted, now if last else heat)

    margins, sums, inverse = exchanged(*surveyed_start(), None)
    solved, rows = fine(local_inverse, rhs, margins)
    lifted = coarse_solve(inverse, sums)
    now, first, final, left, right = updated(solved, lifted, None)
    for sweep in range(ITERS - 1):
        around = edges(first, final, "grp") + edges(left, right, "mem")
        residual, *found = surveyed_residual(now, around)
        margins, sums, inverse = exchanged(*found, inverse)
        solved, rows = fine(rows, residual, margins)
        lifted = coarse_solve(inverse, sums)
        now = updated(solved, lifted, now)[0]
    return now


def solution(mesh):
    placed = (
        P("grp", "mem", None),
        P("grp", "mem"),
        P(("grp", "mem"), None),
        P("grp", "mem", None),
        P(("grp", "mem"), None),
    )
    return jax.shard_map(
        on_device, mesh=mesh, in_specs=placed, out_specs=P("grp", "mem", None), check_vma=False
    )
```

```python
import functools

import jax
import jax.numpy as jnp
from jax import lax
from jax.experimental import pallas as pl
from jax.experimental.pallas import tpu as pltpu
from jax.sharding import PartitionSpec as P

OV = 4
ITERS = 2
HOLD = 6
ORDER = range
LANES = 128
EXACT = lax.Precision.HIGHEST
F32 = jnp.float32
BF16 = jnp.bfloat16


def shifted(value, axis, distance):
    count = lax.axis_size(axis)
    return lax.ppermute(value, axis, [(i, (i + distance) % count) for i in range(count)])


def edges(low_edge, high_edge, axis):
    return beyond(shifted(high_edge, axis, 1), shifted(low_edge, axis, -1), axis)


def beyond(low, high, axis):
    index = lax.axis_index(axis)
    last = lax.axis_size(axis) - 1
    return jnp.where(index == 0, 0, low), jnp.where(index == last, 0, high)


def summed_over_members(shares):
    members = lax.axis_size("mem")
    sizes = [2] * (members.bit_length() - 1)
    shares = shares.reshape(*sizes, shares.shape[0] // members, shares.shape[1])
    for k in ORDER(len(sizes)):
        bit = lax.axis_index("mem") >> k & 1
        axis = len(sizes) - 1 - k
        keep = lax.dynamic_slice_in_dim(shares, bit, 1, axis)
        send = lax.dynamic_slice_in_dim(shares, 1 - bit, 1, axis)
        pairs = [(i, i ^ 1 << k) for i in range(members)]
        shares = keep + lax.ppermute(send, "mem", pairs)
    return shares.reshape(shares.shape[-2:])


def split(values):
    high = values.astype(BF16)
    rest = values - high.astype(F32)
    middle = rest.astype(BF16)
    return high, middle, (rest - middle.astype(F32)).astype(BF16)


def product(a, b):
    return jnp.dot(a, b, preferred_element_type=F32)


def modes_of(basis_ref, first, rows):
    return split(jnp.concatenate([basis_ref[first + k] for k in range(rows)], axis=1))


def restrict(basis_ref, first, block):
    rows, own_y, columns = block.shape
    high, middle, low = modes_of(basis_ref, first, rows)
    modes = high.shape[0]
    block_high, block_middle, block_low = split(block.reshape(rows * own_y, columns))
    three = product(jnp.concatenate([high, middle, low], axis=0), block_high)
    two = product(jnp.concatenate([high, middle], axis=0), block_middle)
    one = product(high, block_low)
    return one + (two[modes:] + three[2 * modes :]) + (two[:modes] + three[modes : 2 * modes]) + three[:modes]


def survey(block, basis_ref, first, down_ref, up_ref, side_ref):
    rows, own_y, columns = block.shape
    count = OV * own_y
    if first == 0:
        down_ref[:count] = block[:OV].reshape(count, columns).astype(BF16)
    if first + rows == side_ref.shape[0]:
        up_ref[:count] = block[rows - OV :].reshape(count, columns).astype(BF16)
    left = lax.broadcasted_iota(jnp.int32, (rows, 2 * OV, columns), 1) < OV
    side_ref[first : first + rows] = jnp.where(
        left, block[:, : 2 * OV], block[:, own_y - 2 * OV :]
    ).astype(BF16)
    return restrict(basis_ref, first, block)


def finish(total, start, down_ref, up_ref, sum_ref):
    sum_ref[...] = total
    parts = jnp.concatenate(split(total), axis=0)
    end = start + parts.shape[0]
    down_ref[start:end] = parts
    up_ref[start:end] = parts
    return end


def start_kernel(
    rhs_ref,
    basis_hbm,
    inverse_hbm,
    down_ref,
    up_ref,
    side_ref,
    sum_ref,
    held,
    basis_ref,
    inverse_ref,
    arrived,
    beside,
):
    own_x, own_y, columns = held.shape
    small = [
        pltpu.make_async_copy(inverse_hbm, inverse_ref, beside.at[0]),
        pltpu.make_async_copy(basis_hbm, basis_ref, beside.at[1]),
    ]
    copies = [
        pltpu.make_async_copy(
            rhs_ref.at[pl.ds(first, OV)], held.at[pl.ds(first, OV)], arrived.at[first // OV]
        )
        for first in range(0, own_x, OV)
    ]
    for copy in small + copies:
        copy.start()
    for copy in small:
        copy.wait()

    groups = lax.axis_size("grp")
    width = inverse_ref.shape[1] // groups
    modes = inverse_ref.shape[0]
    start = OV * own_y + 3 * modes
    for ref, step in ((up_ref, 1), (down_ref, groups - 1)):
        group = lax.rem(lax.axis_index("grp") + step, groups)
        wanted = inverse_ref[:, pl.ds(pl.multiple_of(group * width, width), width)]
        parts = jnp.concatenate(split(wanted), axis=1)
        for k in range(3 * width // columns):
            ref[start + k * modes : start + (k + 1) * modes] = parts[
                :, k * columns : (k + 1) * columns
            ]

    total = jnp.zeros(sum_ref.shape, F32)
    for first in range(0, own_x, OV):
        copies[first // OV].wait()
        block = held[first : first + OV]
        total = total + survey(block, basis_ref, first, down_ref, up_ref, side_ref)
    finish(total, OV * own_y, down_ref, up_ref, sum_ref)


def residual_kernel(
    rhs_ref,
    now_ref,
    below_ref,
    above_ref,
    left_ref,
    right_ref,
    heat_ref,
    basis_ref,
    out_ref,
    down_ref,
    up_ref,
    side_ref,
    sum_ref,
):
    own_x, own_y, columns = now_ref.shape
    place = lax.broadcasted_iota(jnp.int32, (own_y, columns), 0)
    place_heat = place[:, :LANES]

    def flux(values, heat, other, other_heat):
        face = 0.5 * (heat + other_heat)
        return jnp.concatenate([face] * (columns // LANES), axis=1) * (values - other)

    def parts(row):
        return row[:, :columns], row[:, columns:]

    here, heat = now_ref[0], heat_ref[0]
    before = flux(*parts(below_ref[0]), here, heat)
    total = jnp.zeros(sum_ref.shape, F32)
    for index in range(own_x):
        if index + 1 < own_x:
            after, after_heat = now_ref[index + 1], heat_ref[index + 1]
        else:
            after, after_heat = parts(above_ref[0])
        across = flux(here, heat, after, after_heat)
        right, right_heat = parts(right_ref[index // OV, index % OV : index % OV + 1])
        left, left_heat = parts(left_ref[index // OV, index % OV : index % OV + 1])
        right = jnp.where(place == own_y - 1, right, pltpu.roll(here, own_y - 1, 0))
        right_heat = jnp.where(place_heat == own_y - 1, right_heat, pltpu.roll(heat, own_y - 1, 0))
        along = flux(here, heat, right, right_heat)
        entering = jnp.where(
            place == 0, flux(left, left_heat, here[:1], heat[:1]), pltpu.roll(along, 1, 0)
        )
        out_ref[index] = rhs_ref[index] - ((across - before) + (along - entering))
        here, heat, before = after, after_heat, across
        if index % OV == OV - 1:
            first = index + 1 - OV
            block = out_ref[first : first + OV]
            total = total + survey(block, basis_ref, first, down_ref, up_ref, side_ref)
    finish(total, OV * own_y, down_ref, up_ref, sum_ref)


def hold_kernel(inverse_ref, heat_ref, order_ref, out_ref, arrived):
    del heat_ref, order_ref
    count = arrived.shape[0]
    rows = out_ref.shape[0] // count
    skipped = (inverse_ref.shape[0] - out_ref.shape[0]) // 2
    copies = [
        pltpu.make_async_copy(
            inverse_ref.at[pl.ds(skipped + k * rows, rows)],
            out_ref.at[pl.ds(k * rows, rows)],
            arrived.at[k],
        )
        for k in range(count)
    ]
    for copy in copies:
        copy.start()
    for copy in copies:
        copy.wait()


def fine_kernel(rows_ref, block_ref, low_ref, high_ref, side_ref, out_ref, window, wide, solved):
    own_x, own_y, columns = block_ref.shape
    span_y = own_y + 2 * OV
    rows = solved.shape[0] // span_y

    def place(index, values):
        wide[OV : OV + own_y, :] = values
        sides = side_ref[index].astype(F32)
        wide[:OV, :] = sides[:OV]
        wide[OV + own_y :, :] = sides[OV:]
        window[index * span_y : (index + 1) * span_y, :] = wide[...].astype(BF16)

    for index in range(OV):
        place(index, low_ref[index].astype(F32))
        place(OV + own_x + index, high_ref[index].astype(F32))
    for index in range(own_x):
        place(OV + index, block_ref[index])

    for first in range(0, own_x, rows):
        solved[...] = product(
            rows_ref[first * span_y : (first + rows) * span_y, :], window[...]
        )
        for k in range(rows):
            out_ref[first + k] = solved[k * span_y + OV : k * span_y + OV + own_y, :]


def update_kernel(last, fine_ref, basis_ref, lifted_ref, extra_ref, out_ref, *refs):
    own_x, own_y, columns = fine_ref.shape
    if last:
        result, left_for = refs
    else:
        first_ref, last_ref, left_ref, right_ref = refs
        result = out_ref
    high, middle, low = split(lifted_ref[...])
    lifted = jnp.concatenate([high, middle, high, low, middle, high], axis=0)
    sends = []
    for first in range(0, own_x, OV):
        high, middle, low = modes_of(basis_ref, first, OV)
        coarse = lax.dot_general(
            jnp.concatenate([high, high, middle, high, middle, low], axis=0),
            lifted,
            (((0,), (0,)), ((), ())),
            preferred_element_type=F32,
        )
        for k in range(OV):
            value = fine_ref[first + k] + coarse[k * own_y : (k + 1) * own_y]
            if last:
                value = extra_ref[first + k] + value
            result[first + k] = value
        if last:
            sends.append(
                pltpu.make_async_copy(
                    result.at[pl.ds(first, OV)],
                    out_ref.at[pl.ds(first, OV)],
                    left_for.at[first // OV],
                )
            )
            sends[-1].start()
        else:
            for k in range(OV):
                for ref, at in ((left_ref, 0), (right_ref, own_y - 1)):
                    ref[first // OV, k : k + 1, :columns] = result[first + k, at : at + 1]
                    ref[first // OV, k : k + 1, columns:] = extra_ref[first + k, at : at + 1]
    for send in sends:
        send.wait()
    if not last:
        first_ref[0] = jnp.concatenate([result[0], extra_ref[0]], axis=1)
        last_ref[0] = jnp.concatenate([result[own_x - 1], extra_ref[own_x - 1]], axis=1)


def shape_of(shape, kind):
    return jax.ShapeDtypeStruct(shape, kind)


def on_device(rhs, conductivity, local_inverse, coarse_basis, coarse_inverse):
    own_x, own_y, columns = rhs.shape
    modes = coarse_basis.shape[2]
    span_x = own_x + 2 * OV
    span_y = own_y + 2 * OV
    local = span_x * span_y
    basis = jnp.transpose(coarse_basis, (0, 2, 1))
    heat = jnp.broadcast_to(conductivity[:, :, None], (own_x, own_y, LANES))

    def params(mebibytes):
        return pltpu.CompilerParams(vmem_limit_bytes=mebibytes * 2**20)

    group = 2 * OV if own_x % (2 * OV) == 0 else OV
    in_vmem = pl.BlockSpec(memory_space=pltpu.VMEM)
    in_hbm = pl.BlockSpec(memory_space=pltpu.HBM)

    members, groups = lax.axis_size("mem"), lax.axis_size("grp")
    width = members * modes
    edge_rows = OV * own_y
    sum_rows = 3 * modes
    inverse_rows = 3 * width // columns * modes

    def survey_shapes(rows):
        return [
            shape_of((rows, columns), BF16),
            shape_of((rows, columns), BF16),
            shape_of((own_x, 2 * OV, columns), BF16),
            shape_of((modes, columns), F32),
        ]

    def surveyed_start():
        return pl.pallas_call(
            start_kernel,
            in_specs=[in_hbm] * 3,
            out_specs=[in_vmem] * 4,
            out_shape=survey_shapes(edge_rows + sum_rows + inverse_rows),
            scratch_shapes=[
                pltpu.VMEM(rhs.shape, F32),
                pltpu.VMEM(basis.shape, F32),
                pltpu.VMEM(coarse_inverse.shape, F32),
                pltpu.SemaphoreType.DMA((own_x // OV,)),
                pltpu.SemaphoreType.DMA((2,)),
            ],
            compiler_params=params(16),
        )(*(pltpu.with_memory_space_constraint(a, pltpu.HBM) for a in (rhs, basis, coarse_inverse)))

    def surveyed_residual(now, around):
        return pl.pallas_call(
            residual_kernel,
            in_specs=[in_vmem] * 8,
            out_specs=[in_vmem] * 5,
            out_shape=[shape_of(rhs.shape, F32)] + survey_shapes(edge_rows + sum_rows),
            compiler_params=params(16),
        )(rhs, now, *around, heat, basis)

    def added(parts):
        high, middle, low = (part.astype(F32) for part in parts)
        return high + middle + low

    def sums_in(message):
        return added(jnp.split(message[edge_rows : edge_rows + sum_rows], 3, axis=0))

    def inverse_in(message):
        pieces = message[edge_rows + sum_rows :]
        pieces = jnp.concatenate(jnp.split(pieces, inverse_rows // modes, axis=0), axis=1)
        return added(jnp.split(pieces, 3, axis=1))

    def inverse_for(distance):
        group = (lax.axis_index("grp") + distance) % groups
        return lax.dynamic_slice_in_dim(coarse_inverse, group * width, width, 1)

    def exchanged(down, up, sides, restricted, inverse):
        first = inverse is None
        from_below, from_above = shifted(up, "grp", 1), shifted(down, "grp", -1)
        sums = [restricted]
        rows = [inverse_for(0)]
        for distance in range(2, groups - 1):
            if first:
                message = jnp.concatenate([restricted, inverse_for(distance)], axis=1)
            else:
                message = restricted
            message = shifted(message, "grp", distance)
            sums.append(message[:, :columns])
            rows.append(message[:, columns:])
        for message in (from_below, from_above):
            sums.append(sums_in(message))
            if first:
                rows.append(inverse_in(message))
        if first:
            inverse = jnp.concatenate(rows, axis=0)
        low, high = beyond(from_below[:edge_rows], from_above[:edge_rows], "grp")
        low = low.reshape(OV, own_y, columns)
        high = high.reshape(OV, own_y, columns)
        corners = [jnp.concatenate([m[:, :OV], m[:, -OV:]], axis=1) for m in (low, high)]
        sides = jnp.concatenate([corners[0], sides, corners[1]], axis=0)
        left, right = edges(sides[:, :OV], sides[:, OV:], "mem")
        margins = low, high, jnp.concatenate([left, right], axis=1)
        return margins, jnp.concatenate(sums, axis=0), inverse

    def coarse_solve(inverse, sums):
        shares = lax.dot_general(
            inverse,
            sums,
            (((0,), (0,)), ((), ())),
            precision=EXACT,
            preferred_element_type=F32,
        )
        return summed_over_members(shares)

    held = (own_x * span_y, local)

    def held_rows(order):
        return pl.pallas_call(
            hold_kernel,
            in_specs=[in_hbm, pl.BlockSpec(memory_space=pl.ANY), pl.BlockSpec(memory_space=pl.ANY)],
            out_specs=in_vmem,
            out_shape=shape_of(held, BF16),
            scratch_shapes=[pltpu.SemaphoreType.DMA((HOLD,))],
            compiler_params=params(8),
            cost_estimate=pl.CostEstimate(
                flops=0, bytes_accessed=4 * held[0] * local, transcendentals=0
            ),
        )(pltpu.with_memory_space_constraint(local_inverse, pltpu.HBM), heat, order)

    def fine(rows, values, margins):
        return pl.pallas_call(
            fine_kernel,
            in_specs=[in_vmem] * 5,
            out_specs=in_vmem,
            out_shape=shape_of(rhs.shape, F32),
            scratch_shapes=[
                pltpu.VMEM((local, columns), BF16),
                pltpu.VMEM((span_y, columns), F32),
                pltpu.VMEM((group * span_y, columns), F32),
            ],
            compiler_params=params(24),
            cost_estimate=pl.CostEstimate(
                flops=2 * held[0] * local * columns,
                bytes_accessed=2 * held[0] * local,
                transcendentals=0,
            ),
        )(rows, values, *margins)

    def updated(solved, lifted, now):
        last = now is not None
        edge = columns + LANES
        out_shape = [shape_of(rhs.shape, F32)]
        if last:
            out_specs = [in_hbm]
            scratch = [pltpu.VMEM(rhs.shape, F32), pltpu.SemaphoreType.DMA((own_x // OV,))]
        else:
            out_specs = [in_vmem] * 5
            out_shape += [shape_of((1, own_y, edge), F32)] * 2
            out_shape += [shape_of((own_x // OV, OV, edge), F32)] * 2
            scratch = []
        return pl.pallas_call(
            functools.partial(update_kernel, last),
            in_specs=[in_vmem] * 4,
            out_specs=out_specs,
            out_shape=out_shape,
            scratch_shapes=scratch,
            compiler_params=params(16),
        )(solved, basis, lifted, now if last else heat)

    found = surveyed_start()
    rows = held_rows(found[-1])
    margins, sums, inverse = exchanged(*found, None)
    solved = fine(rows, rhs, margins)
    lifted = coarse_solve(inverse, sums)
    now, first, final, left, right = updated(solved, lifted, None)
    for sweep in range(ITERS - 1):
        around = edges(first, final, "grp") + edges(left, right, "mem")
        residual, *found = surveyed_residual(now, around)
        margins, sums, inverse = exchanged(*found, inverse)
        solved = fine(rows, residual, margins)
        lifted = coarse_solve(inverse, sums)
        now = updated(solved, lifted, now)[0]
    return now


def solution(mesh):
    placed = (
        P("grp", "mem", None),
        P("grp", "mem"),
        P(("grp", "mem"), None),
        P("grp", "mem", None),
        P(("grp", "mem"), None),
    )
    return jax.shard_map(
        on_device, mesh=mesh, in_specs=placed, out_specs=P("grp", "mem", None), check_vma=False
    )
```

```python
import functools

import jax
import jax.numpy as jnp
from jax import lax
from jax.experimental import pallas as pl
from jax.experimental.pallas import tpu as pltpu
from jax.sharding import PartitionSpec as P

OV = 4
ITERS = 2
HOLD = 6
LANES = 128
EXACT = lax.Precision.HIGHEST
F32 = jnp.float32
BF16 = jnp.bfloat16


def shifted(value, axis, distance):
    count = lax.axis_size(axis)
    return lax.ppermute(value, axis, [(i, (i + distance) % count) for i in range(count)])


def edges(low_edge, high_edge, axis):
    return beyond(shifted(high_edge, axis, 1), shifted(low_edge, axis, -1), axis)


def beyond(low, high, axis):
    index = lax.axis_index(axis)
    last = lax.axis_size(axis) - 1
    return jnp.where(index == 0, 0, low), jnp.where(index == last, 0, high)


def summed_over_members(shares):
    members = lax.axis_size("mem")
    sizes = [2] * (members.bit_length() - 1)
    shares = shares.reshape(*sizes, shares.shape[0] // members, shares.shape[1])
    for k in (*range(1, len(sizes)), 0):
        bit = lax.axis_index("mem") >> k & 1
        axis = len(sizes) - 1 - k
        keep = lax.dynamic_slice_in_dim(shares, bit, 1, axis)
        send = lax.dynamic_slice_in_dim(shares, 1 - bit, 1, axis)
        pairs = [(i, i ^ 1 << k) for i in range(members)]
        shares = keep + lax.ppermute(send, "mem", pairs)
    return shares.reshape(shares.shape[-2:])


def split(values):
    high = values.astype(BF16)
    rest = values - high.astype(F32)
    middle = rest.astype(BF16)
    return high, middle, (rest - middle.astype(F32)).astype(BF16)


def product(a, b):
    return jnp.dot(a, b, preferred_element_type=F32)


def modes_of(basis_ref, first, rows):
    return split(jnp.concatenate([basis_ref[first + k] for k in range(rows)], axis=1))


def restrict(basis_ref, first, block):
    rows, own_y, columns = block.shape
    return weighted(modes_of(basis_ref, first, rows), block.reshape(rows * own_y, columns))


def weighted(weights, cells):
    high, middle, low = weights
    modes = high.shape[0]
    block_high, block_middle, block_low = split(cells)
    three = product(jnp.concatenate([high, middle, low], axis=0), block_high)
    two = product(jnp.concatenate([high, middle], axis=0), block_middle)
    one = product(high, block_low)
    return one + (two[modes:] + three[2 * modes :]) + (two[:modes] + three[modes : 2 * modes]) + three[:modes]


def survey(block, basis_ref, first, down_ref, up_ref, side_ref):
    rows, own_y, columns = block.shape
    count = OV * own_y
    if first == 0:
        down_ref[:count] = block[:OV].reshape(count, columns).astype(BF16)
    if first + rows == side_ref.shape[0]:
        up_ref[:count] = block[rows - OV :].reshape(count, columns).astype(BF16)
    left = lax.broadcasted_iota(jnp.int32, (rows, 2 * OV, columns), 1) < OV
    side_ref[first : first + rows] = jnp.where(
        left, block[:, : 2 * OV], block[:, own_y - 2 * OV :]
    ).astype(BF16)
    return restrict(basis_ref, first, block)


def finish(total, start, down_ref, up_ref, sum_ref):
    sum_ref[...] = total
    parts = jnp.concatenate(split(total), axis=0)
    end = start + parts.shape[0]
    down_ref[start:end] = parts
    up_ref[start:end] = parts
    return end


def start_kernel(
    rhs_ref,
    basis_hbm,
    inverse_hbm,
    down_ref,
    up_ref,
    side_ref,
    sum_ref,
    held,
    basis_ref,
    inverse_ref,
    arrived,
    beside,
):
    own_x, own_y, columns = held.shape
    small = [
        pltpu.make_async_copy(inverse_hbm, inverse_ref, beside.at[0]),
        pltpu.make_async_copy(basis_hbm, basis_ref, beside.at[1]),
    ]
    copies = [
        pltpu.make_async_copy(
            rhs_ref.at[pl.ds(first, OV)], held.at[pl.ds(first, OV)], arrived.at[first // OV]
        )
        for first in range(0, own_x, OV)
    ]
    for copy in small + copies:
        copy.start()
    for copy in small:
        copy.wait()

    groups = lax.axis_size("grp")
    width = inverse_ref.shape[1] // groups
    modes = inverse_ref.shape[0]
    start = OV * own_y + 3 * modes
    for ref, step in ((up_ref, 1), (down_ref, groups - 1)):
        group = lax.rem(lax.axis_index("grp") + step, groups)
        wanted = inverse_ref[:, pl.ds(pl.multiple_of(group * width, width), width)]
        parts = jnp.concatenate(split(wanted), axis=1)
        for k in range(3 * width // columns):
            ref[start + k * modes : start + (k + 1) * modes] = parts[
                :, k * columns : (k + 1) * columns
            ]

    total = jnp.zeros(sum_ref.shape, F32)
    for first in range(0, own_x, OV):
        copies[first // OV].wait()
        block = held[first : first + OV]
        total = total + survey(block, basis_ref, first, down_ref, up_ref, side_ref)
    finish(total, OV * own_y, down_ref, up_ref, sum_ref)


def flux(values, heat, other, other_heat):
    face = 0.5 * (heat + other_heat)
    return jnp.concatenate([face] * (values.shape[1] // LANES), axis=1) * (values - other)


def inner_kernel(rhs_ref, now_ref, heat_ref, basis_ref, out_ref, sum_ref, modes_ref):
    own_x, own_y, columns = now_ref.shape
    place = lax.broadcasted_iota(jnp.int32, (own_y, columns), 0)
    here, heat = now_ref[0], heat_ref[0]
    before = jnp.zeros((own_y, columns), F32)
    total = jnp.zeros(sum_ref.shape, F32)
    for index in range(own_x):
        if index + 1 < own_x:
            after, after_heat = now_ref[index + 1], heat_ref[index + 1]
            across = flux(here, heat, after, after_heat)
        else:
            across = jnp.zeros((own_y, columns), F32)
        along = flux(here, heat, pltpu.roll(here, own_y - 1, 0), pltpu.roll(heat, own_y - 1, 0))
        along = jnp.where(place == own_y - 1, 0.0, along)
        entering = pltpu.roll(along, 1, 0)
        out_ref[index] = rhs_ref[index] - ((across - before) + (along - entering))
        here, heat, before = after, after_heat, across
        if index % OV == OV - 1:
            first = index + 1 - OV
            total = total + restrict(basis_ref, first, out_ref[first : first + OV])
    sum_ref[...] = total
    sides = []
    for index in range(own_x):
        row = basis_ref[index]
        left = lax.broadcasted_iota(jnp.int32, (row.shape[0], 2 * OV), 1) < OV
        sides.append(jnp.where(left, row[:, : 2 * OV], row[:, own_y - 2 * OV :]))
    modes_ref[...] = jnp.concatenate([basis_ref[0], basis_ref[own_x - 1], *sides], axis=1)


def edge_kernel(
    part_ref,
    now_ref,
    below_ref,
    above_ref,
    left_ref,
    right_ref,
    heat_ref,
    part_sum_ref,
    modes_ref,
    out_ref,
    down_ref,
    up_ref,
    side_ref,
    sum_ref,
    changes,
):
    del part_ref
    own_x, own_y, columns = now_ref.shape
    count = OV * own_y
    sides = 2 * OV

    def parts(row):
        return row[:, :columns], row[:, columns:]

    for at, index, ref in ((0, 0, below_ref), (own_y, own_x - 1, above_ref)):
        change = flux(*parts(ref[0]), now_ref[index], heat_ref[index])
        changes[at : at + own_y] = change
        out_ref[index] = out_ref[index] + change
    place = lax.broadcasted_iota(jnp.int32, (sides, columns), 0)
    for index in range(own_x):
        tiles = []
        for ref, start, cell in ((left_ref, 0, 0), (right_ref, own_y - sides, sides - 1)):
            other = parts(ref[index // OV, index % OV : index % OV + 1])
            tile = slice(start, start + sides)
            change = flux(*other, now_ref[index, tile], heat_ref[index, tile])
            change = jnp.where(place == cell, change, 0.0)
            tiles.append(change)
            out_ref[index, tile] = out_ref[index, tile] + change
        at = 2 * own_y + index * sides
        changes[at : at + sides] = tiles[0] + tiles[1]
        side_ref[index] = jnp.where(
            place < OV, out_ref[index, :sides], out_ref[index, own_y - sides :]
        ).astype(BF16)
    down_ref[:count] = out_ref[:OV].reshape(count, columns).astype(BF16)
    up_ref[:count] = out_ref[own_x - OV :].reshape(count, columns).astype(BF16)
    total = part_sum_ref[...] + weighted(split(modes_ref[...]), changes[...])
    finish(total, count, down_ref, up_ref, sum_ref)


def hold_kernel(inverse_ref, heat_ref, order_ref, out_ref, arrived):
    del heat_ref, order_ref
    count = arrived.shape[0]
    rows = out_ref.shape[0] // count
    skipped = (inverse_ref.shape[0] - out_ref.shape[0]) // 2
    copies = [
        pltpu.make_async_copy(
            inverse_ref.at[pl.ds(skipped + k * rows, rows)],
            out_ref.at[pl.ds(k * rows, rows)],
            arrived.at[k],
        )
        for k in range(count)
    ]
    for copy in copies:
        copy.start()
    for copy in copies:
        copy.wait()


def fine_kernel(rows_ref, block_ref, low_ref, high_ref, side_ref, out_ref, window, wide, solved):
    own_x, own_y, columns = block_ref.shape
    span_y = own_y + 2 * OV
    rows = solved.shape[0] // span_y

    def place(index, values):
        wide[OV : OV + own_y, :] = values
        sides = side_ref[index].astype(F32)
        wide[:OV, :] = sides[:OV]
        wide[OV + own_y :, :] = sides[OV:]
        window[index * span_y : (index + 1) * span_y, :] = wide[...].astype(BF16)

    for index in range(OV):
        place(index, low_ref[index].astype(F32))
        place(OV + own_x + index, high_ref[index].astype(F32))
    for index in range(own_x):
        place(OV + index, block_ref[index])

    for first in range(0, own_x, rows):
        solved[...] = product(
            rows_ref[first * span_y : (first + rows) * span_y, :], window[...]
        )
        for k in range(rows):
            out_ref[first + k] = solved[k * span_y + OV : k * span_y + OV + own_y, :]


def update_kernel(last, fine_ref, basis_ref, lifted_ref, extra_ref, out_ref, *refs):
    own_x, own_y, columns = fine_ref.shape
    if last:
        result, left_for = refs
    else:
        first_ref, last_ref, left_ref, right_ref = refs
        result = out_ref
    high, middle, low = split(lifted_ref[...])
    lifted = jnp.concatenate([high, middle, high, low, middle, high], axis=0)
    sends = []
    for first in range(0, own_x, OV):
        high, middle, low = modes_of(basis_ref, first, OV)
        coarse = lax.dot_general(
            jnp.concatenate([high, high, middle, high, middle, low], axis=0),
            lifted,
            (((0,), (0,)), ((), ())),
            preferred_element_type=F32,
        )
        for k in range(OV):
            value = fine_ref[first + k] + coarse[k * own_y : (k + 1) * own_y]
            if last:
                value = extra_ref[first + k] + value
            result[first + k] = value
        if last:
            sends.append(
                pltpu.make_async_copy(
                    result.at[pl.ds(first, OV)],
                    out_ref.at[pl.ds(first, OV)],
                    left_for.at[first // OV],
                )
            )
            sends[-1].start()
        else:
            for k in range(OV):
                for ref, at in ((left_ref, 0), (right_ref, own_y - 1)):
                    ref[first // OV, k : k + 1, :columns] = result[first + k, at : at + 1]
                    ref[first // OV, k : k + 1, columns:] = extra_ref[first + k, at : at + 1]
    for send in sends:
        send.wait()
    if not last:
        first_ref[0] = jnp.concatenate([result[0], extra_ref[0]], axis=1)
        last_ref[0] = jnp.concatenate([result[own_x - 1], extra_ref[own_x - 1]], axis=1)


def shape_of(shape, kind):
    return jax.ShapeDtypeStruct(shape, kind)


def on_device(rhs, conductivity, local_inverse, coarse_basis, coarse_inverse):
    own_x, own_y, columns = rhs.shape
    modes = coarse_basis.shape[2]
    span_x = own_x + 2 * OV
    span_y = own_y + 2 * OV
    local = span_x * span_y
    basis = jnp.transpose(coarse_basis, (0, 2, 1))
    heat = jnp.broadcast_to(conductivity[:, :, None], (own_x, own_y, LANES))

    def params(mebibytes):
        return pltpu.CompilerParams(vmem_limit_bytes=mebibytes * 2**20)

    group = 2 * OV if own_x % (2 * OV) == 0 else OV
    in_vmem = pl.BlockSpec(memory_space=pltpu.VMEM)
    in_hbm = pl.BlockSpec(memory_space=pltpu.HBM)

    members, groups = lax.axis_size("mem"), lax.axis_size("grp")
    width = members * modes
    edge_rows = OV * own_y
    sum_rows = 3 * modes
    inverse_rows = 3 * width // columns * modes

    def survey_shapes(rows):
        return [
            shape_of((rows, columns), BF16),
            shape_of((rows, columns), BF16),
            shape_of((own_x, 2 * OV, columns), BF16),
            shape_of((modes, columns), F32),
        ]

    def surveyed_start():
        return pl.pallas_call(
            start_kernel,
            in_specs=[in_hbm] * 3,
            out_specs=[in_vmem] * 4,
            out_shape=survey_shapes(edge_rows + sum_rows + inverse_rows),
            scratch_shapes=[
                pltpu.VMEM(rhs.shape, F32),
                pltpu.VMEM(basis.shape, F32),
                pltpu.VMEM(coarse_inverse.shape, F32),
                pltpu.SemaphoreType.DMA((own_x // OV,)),
                pltpu.SemaphoreType.DMA((2,)),
            ],
            compiler_params=params(16),
        )(*(pltpu.with_memory_space_constraint(a, pltpu.HBM) for a in (rhs, basis, coarse_inverse)))

    edge_cells = 2 * own_y + 2 * OV * own_x

    def inner(now):
        return pl.pallas_call(
            inner_kernel,
            in_specs=[in_vmem] * 4,
            out_specs=[in_vmem] * 3,
            out_shape=[
                shape_of(rhs.shape, F32),
                shape_of((modes, columns), F32),
                shape_of((modes, edge_cells), F32),
            ],
            compiler_params=params(16),
            cost_estimate=pl.CostEstimate(
                flops=0, bytes_accessed=12 * own_x * own_y * columns, transcendentals=0
            ),
        )(rhs, now, heat, basis)

    def surveyed_residual(now, around):
        part, part_sum, edge_modes = inner(now)
        return pl.pallas_call(
            edge_kernel,
            in_specs=[in_vmem] * 9,
            out_specs=[in_vmem] * 5,
            out_shape=[shape_of(rhs.shape, F32)] + survey_shapes(edge_rows + sum_rows),
            scratch_shapes=[pltpu.VMEM((edge_cells, columns), F32)],
            input_output_aliases={0: 0},
            compiler_params=params(16),
        )(part, now, *around, heat, part_sum, edge_modes)

    def added(parts):
        high, middle, low = (part.astype(F32) for part in parts)
        return high + middle + low

    def sums_in(message):
        return added(jnp.split(message[edge_rows : edge_rows + sum_rows], 3, axis=0))

    def inverse_in(message):
        pieces = message[edge_rows + sum_rows :]
        pieces = jnp.concatenate(jnp.split(pieces, inverse_rows // modes, axis=0), axis=1)
        return added(jnp.split(pieces, 3, axis=1))

    def inverse_for(distance):
        group = (lax.axis_index("grp") + distance) % groups
        return lax.dynamic_slice_in_dim(coarse_inverse, group * width, width, 1)

    def exchanged(down, up, sides, restricted, inverse):
        first = inverse is None
        from_below, from_above = shifted(up, "grp", 1), shifted(down, "grp", -1)
        sums = [restricted]
        rows = [inverse_for(0)]
        for distance in range(2, groups - 1):
            if first:
                message = jnp.concatenate([restricted, inverse_for(distance)], axis=1)
            else:
                message = restricted
            message = shifted(message, "grp", distance)
            sums.append(message[:, :columns])
            rows.append(message[:, columns:])
        for message in (from_below, from_above):
            sums.append(sums_in(message))
            if first:
                rows.append(inverse_in(message))
        if first:
            inverse = jnp.concatenate(rows, axis=0)
        low, high = beyond(from_below[:edge_rows], from_above[:edge_rows], "grp")
        low = low.reshape(OV, own_y, columns)
        high = high.reshape(OV, own_y, columns)
        corners = [jnp.concatenate([m[:, :OV], m[:, -OV:]], axis=1) for m in (low, high)]
        sides = jnp.concatenate([corners[0], sides, corners[1]], axis=0)
        left, right = edges(sides[:, :OV], sides[:, OV:], "mem")
        margins = low, high, jnp.concatenate([left, right], axis=1)
        return margins, jnp.concatenate(sums, axis=0), inverse

    def coarse_solve(inverse, sums):
        shares = lax.dot_general(
            inverse,
            sums,
            (((0,), (0,)), ((), ())),
            precision=EXACT,
            preferred_element_type=F32,
        )
        return summed_over_members(shares)

    held = (own_x * span_y, local)

    def held_rows(order):
        return pl.pallas_call(
            hold_kernel,
            in_specs=[in_hbm, pl.BlockSpec(memory_space=pl.ANY), pl.BlockSpec(memory_space=pl.ANY)],
            out_specs=in_vmem,
            out_shape=shape_of(held, BF16),
            scratch_shapes=[pltpu.SemaphoreType.DMA((HOLD,))],
            compiler_params=params(8),
            cost_estimate=pl.CostEstimate(
                flops=0, bytes_accessed=4 * held[0] * local, transcendentals=0
            ),
        )(pltpu.with_memory_space_constraint(local_inverse, pltpu.HBM), heat, order)

    def fine(rows, values, margins):
        return pl.pallas_call(
            fine_kernel,
            in_specs=[in_vmem] * 5,
            out_specs=in_vmem,
            out_shape=shape_of(rhs.shape, F32),
            scratch_shapes=[
                pltpu.VMEM((local, columns), BF16),
                pltpu.VMEM((span_y, columns), F32),
                pltpu.VMEM((group * span_y, columns), F32),
            ],
            compiler_params=params(24),
            cost_estimate=pl.CostEstimate(
                flops=2 * held[0] * local * columns,
                bytes_accessed=2 * held[0] * local,
                transcendentals=0,
            ),
        )(rows, values, *margins)

    def updated(solved, lifted, now):
        last = now is not None
        edge = columns + LANES
        out_shape = [shape_of(rhs.shape, F32)]
        if last:
            out_specs = [in_hbm]
            scratch = [pltpu.VMEM(rhs.shape, F32), pltpu.SemaphoreType.DMA((own_x // OV,))]
        else:
            out_specs = [in_vmem] * 5
            out_shape += [shape_of((1, own_y, edge), F32)] * 2
            out_shape += [shape_of((own_x // OV, OV, edge), F32)] * 2
            scratch = []
        return pl.pallas_call(
            functools.partial(update_kernel, last),
            in_specs=[in_vmem] * 4,
            out_specs=out_specs,
            out_shape=out_shape,
            scratch_shapes=scratch,
            compiler_params=params(16),
        )(solved, basis, lifted, now if last else heat)

    found = surveyed_start()
    rows = held_rows(found[-1])
    margins, sums, inverse = exchanged(*found, None)
    solved = fine(rows, rhs, margins)
    lifted = coarse_solve(inverse, sums)
    now, first, final, left, right = updated(solved, lifted, None)
    for sweep in range(ITERS - 1):
        around = edges(first, final, "grp") + edges(left, right, "mem")
        residual, *found = surveyed_residual(now, around)
        margins, sums, inverse = exchanged(*found, inverse)
        solved = fine(rows, residual, margins)
        lifted = coarse_solve(inverse, sums)
        now = updated(solved, lifted, now)[0]
    return now


def solution(mesh):
    placed = (
        P("grp", "mem", None),
        P("grp", "mem"),
        P(("grp", "mem"), None),
        P("grp", "mem", None),
        P(("grp", "mem"), None),
    )
    return jax.shard_map(
        on_device, mesh=mesh, in_specs=placed, out_specs=P("grp", "mem", None), check_vma=False
    )
```

```python
import functools

import jax
import jax.numpy as jnp
from jax import lax
from jax.experimental import pallas as pl
from jax.experimental.pallas import tpu as pltpu
from jax.sharding import PartitionSpec as P

OV = 4
ITERS = 2
LANES = 128
EXACT = lax.Precision.HIGHEST
F32 = jnp.float32
BF16 = jnp.bfloat16


def shifted(value, axis, distance):
    count = lax.axis_size(axis)
    return lax.ppermute(value, axis, [(i, (i + distance) % count) for i in range(count)])


def edges(low_edge, high_edge, axis):
    return beyond(shifted(high_edge, axis, 1), shifted(low_edge, axis, -1), axis)


def beyond(low, high, axis):
    index = lax.axis_index(axis)
    last = lax.axis_size(axis) - 1
    return jnp.where(index == 0, 0, low), jnp.where(index == last, 0, high)


def summed_over_members(shares):
    members = lax.axis_size("mem")
    sizes = [2] * (members.bit_length() - 1)
    shares = shares.reshape(*sizes, shares.shape[0] // members, shares.shape[1])
    for k in (*range(1, len(sizes)), 0):
        bit = lax.axis_index("mem") >> k & 1
        axis = len(sizes) - 1 - k
        keep = lax.dynamic_slice_in_dim(shares, bit, 1, axis)
        send = lax.dynamic_slice_in_dim(shares, 1 - bit, 1, axis)
        pairs = [(i, i ^ 1 << k) for i in range(members)]
        shares = keep + lax.ppermute(send, "mem", pairs)
    return shares.reshape(shares.shape[-2:])


def split(values):
    high = values.astype(BF16)
    rest = values - high.astype(F32)
    middle = rest.astype(BF16)
    return high, middle, (rest - middle.astype(F32)).astype(BF16)


def product(a, b):
    return jnp.dot(a, b, preferred_element_type=F32)


def modes_of(basis_ref, first, rows):
    return split(jnp.concatenate([basis_ref[first + k] for k in range(rows)], axis=1))


def restrict(basis_ref, first, block):
    rows, own_y, columns = block.shape
    return weighted(modes_of(basis_ref, first, rows), block.reshape(rows * own_y, columns))


def weighted(weights, cells):
    high, middle, low = weights
    modes = high.shape[0]
    block_high, block_middle, block_low = split(cells)
    three = product(jnp.concatenate([high, middle, low], axis=0), block_high)
    two = product(jnp.concatenate([high, middle], axis=0), block_middle)
    one = product(high, block_low)
    return one + (two[modes:] + three[2 * modes :]) + (two[:modes] + three[modes : 2 * modes]) + three[:modes]


def survey(block, basis_ref, first, down_ref, up_ref, side_ref):
    rows, own_y, columns = block.shape
    count = OV * own_y
    if first == 0:
        down_ref[:count] = block[:OV].reshape(count, columns).astype(BF16)
    if first + rows == side_ref.shape[0]:
        up_ref[:count] = block[rows - OV :].reshape(count, columns).astype(BF16)
    left = lax.broadcasted_iota(jnp.int32, (rows, 2 * OV, columns), 1) < OV
    side_ref[first : first + rows] = jnp.where(
        left, block[:, : 2 * OV], block[:, own_y - 2 * OV :]
    ).astype(BF16)
    return restrict(basis_ref, first, block)


def finish(total, start, down_ref, up_ref, sum_ref):
    sum_ref[...] = total
    parts = jnp.concatenate(split(total)[:2], axis=0)
    end = start + parts.shape[0]
    down_ref[start:end] = parts
    up_ref[start:end] = parts


def start_kernel(
    rhs_ref,
    basis_hbm,
    inverse_hbm,
    down_ref,
    up_ref,
    side_ref,
    sum_ref,
    held,
    basis_ref,
    inverse_ref,
    arrived,
    beside,
):
    own_x, own_y, columns = held.shape
    small = [
        pltpu.make_async_copy(inverse_hbm, inverse_ref, beside.at[0]),
        pltpu.make_async_copy(basis_hbm, basis_ref, beside.at[1]),
    ]
    copies = [
        pltpu.make_async_copy(
            rhs_ref.at[pl.ds(first, OV)], held.at[pl.ds(first, OV)], arrived.at[first // OV]
        )
        for first in range(0, own_x, OV)
    ]
    for copy in small + copies:
        copy.start()
    for copy in small:
        copy.wait()

    groups = lax.axis_size("grp")
    width = inverse_ref.shape[1] // groups
    modes = inverse_ref.shape[0]
    start = OV * own_y + 2 * modes
    for ref, step in ((up_ref, 1), (down_ref, groups - 1)):
        group = lax.rem(lax.axis_index("grp") + step, groups)
        wanted = inverse_ref[:, pl.ds(pl.multiple_of(group * width, width), width)]
        parts = jnp.concatenate(split(wanted), axis=1)
        for k in range(3 * width // columns):
            ref[start + k * modes : start + (k + 1) * modes] = parts[
                :, k * columns : (k + 1) * columns
            ]

    total = jnp.zeros(sum_ref.shape, F32)
    for first in range(0, own_x, OV):
        copies[first // OV].wait()
        block = held[first : first + OV]
        total = total + survey(block, basis_ref, first, down_ref, up_ref, side_ref)
    finish(total, OV * own_y, down_ref, up_ref, sum_ref)


def flux(values, heat, other, other_heat):
    face = 0.5 * (heat + other_heat)
    return jnp.concatenate([face] * (values.shape[1] // LANES), axis=1) * (values - other)


def inner_kernel(rhs_ref, now_ref, heat_ref, basis_ref, out_ref, sum_ref, modes_ref):
    own_x, own_y, columns = now_ref.shape
    place = lax.broadcasted_iota(jnp.int32, (own_y, columns), 0)
    here, heat = now_ref[0], heat_ref[0]
    before = jnp.zeros((own_y, columns), F32)
    total = jnp.zeros(sum_ref.shape, F32)
    for index in range(own_x):
        if index + 1 < own_x:
            after, after_heat = now_ref[index + 1], heat_ref[index + 1]
            across = flux(here, heat, after, after_heat)
        else:
            across = jnp.zeros((own_y, columns), F32)
        along = flux(here, heat, pltpu.roll(here, own_y - 1, 0), pltpu.roll(heat, own_y - 1, 0))
        along = jnp.where(place == own_y - 1, 0.0, along)
        entering = pltpu.roll(along, 1, 0)
        out_ref[index] = rhs_ref[index] - ((across - before) + (along - entering))
        here, heat, before = after, after_heat, across
        if index % OV == OV - 1:
            first = index + 1 - OV
            total = total + restrict(basis_ref, first, out_ref[first : first + OV])
    sum_ref[...] = total
    sides = []
    for index in range(own_x):
        row = basis_ref[index]
        left = lax.broadcasted_iota(jnp.int32, (row.shape[0], 2 * OV), 1) < OV
        sides.append(jnp.where(left, row[:, : 2 * OV], row[:, own_y - 2 * OV :]))
    modes_ref[...] = jnp.concatenate([basis_ref[0], basis_ref[own_x - 1], *sides], axis=1)


def edge_kernel(
    part_ref,
    now_ref,
    below_ref,
    above_ref,
    left_ref,
    right_ref,
    heat_ref,
    part_sum_ref,
    modes_ref,
    out_ref,
    down_ref,
    up_ref,
    side_ref,
    sum_ref,
    changes,
):
    del part_ref
    own_x, own_y, columns = now_ref.shape
    count = OV * own_y
    sides = 2 * OV

    def parts(row):
        return row[:, :columns], row[:, columns:]

    for at, index, ref in ((0, 0, below_ref), (own_y, own_x - 1, above_ref)):
        change = flux(*parts(ref[0]), now_ref[index], heat_ref[index])
        changes[at : at + own_y] = change
        out_ref[index] = out_ref[index] + change
    place = lax.broadcasted_iota(jnp.int32, (sides, columns), 0)
    for index in range(own_x):
        tiles = []
        for ref, start, cell in ((left_ref, 0, 0), (right_ref, own_y - sides, sides - 1)):
            other = parts(ref[index // OV, index % OV : index % OV + 1])
            tile = slice(start, start + sides)
            change = flux(*other, now_ref[index, tile], heat_ref[index, tile])
            change = jnp.where(place == cell, change, 0.0)
            tiles.append(change)
            out_ref[index, tile] = out_ref[index, tile] + change
        at = 2 * own_y + index * sides
        changes[at : at + sides] = tiles[0] + tiles[1]
        side_ref[index] = jnp.where(
            place < OV, out_ref[index, :sides], out_ref[index, own_y - sides :]
        ).astype(BF16)
    down_ref[:count] = out_ref[:OV].reshape(count, columns).astype(BF16)
    up_ref[:count] = out_ref[own_x - OV :].reshape(count, columns).astype(BF16)
    total = part_sum_ref[...] + weighted(split(modes_ref[...]), changes[...])
    finish(total, count, down_ref, up_ref, sum_ref)


def hold_kernel(inverse_ref, heat_ref, order_ref, out_ref, arrived):
    del heat_ref, order_ref
    count = arrived.shape[0]
    rows = out_ref.shape[0] // count
    skipped = (inverse_ref.shape[0] - out_ref.shape[0]) // 2
    copies = [
        pltpu.make_async_copy(
            inverse_ref.at[pl.ds(skipped + k * rows, rows)],
            out_ref.at[pl.ds(k * rows, rows)],
            arrived.at[k],
        )
        for k in range(count)
    ]
    for copy in copies:
        copy.start()
    for copy in copies:
        copy.wait()


def fine_kernel(rows_ref, block_ref, low_ref, high_ref, side_ref, out_ref, window, wide, solved):
    own_x, own_y, columns = block_ref.shape
    span_y = own_y + 2 * OV
    rows = solved.shape[0] // span_y

    def place(index, values):
        wide[OV : OV + own_y, :] = values
        sides = side_ref[index].astype(F32)
        wide[:OV, :] = sides[:OV]
        wide[OV + own_y :, :] = sides[OV:]
        window[index * span_y : (index + 1) * span_y, :] = wide[...].astype(BF16)

    for index in range(OV):
        place(index, low_ref[index].astype(F32))
        place(OV + own_x + index, high_ref[index].astype(F32))
    for index in range(own_x):
        place(OV + index, block_ref[index])

    for first in range(0, own_x, rows):
        solved[...] = product(
            rows_ref[first * span_y : (first + rows) * span_y, :], window[...]
        )
        for k in range(rows):
            out_ref[first + k] = solved[k * span_y + OV : k * span_y + OV + own_y, :]


def update_kernel(last, fine_ref, basis_ref, lifted_ref, extra_ref, out_ref, *refs):
    own_x, own_y, columns = fine_ref.shape
    if last:
        result, left_for = refs
    else:
        first_ref, last_ref, left_ref, right_ref = refs
        result = out_ref
    high, middle, low = split(lifted_ref[...])
    lifted = jnp.concatenate([high, middle, high, low, middle, high], axis=0)
    sends = []
    for first in range(0, own_x, OV):
        high, middle, low = modes_of(basis_ref, first, OV)
        coarse = lax.dot_general(
            jnp.concatenate([high, high, middle, high, middle, low], axis=0),
            lifted,
            (((0,), (0,)), ((), ())),
            preferred_element_type=F32,
        )
        for k in range(OV):
            value = fine_ref[first + k] + coarse[k * own_y : (k + 1) * own_y]
            if last:
                value = extra_ref[first + k] + value
            result[first + k] = value
        if last:
            sends.append(
                pltpu.make_async_copy(
                    result.at[pl.ds(first, OV)],
                    out_ref.at[pl.ds(first, OV)],
                    left_for.at[first // OV],
                )
            )
            sends[-1].start()
        else:
            for k in range(OV):
                for ref, at in ((left_ref, 0), (right_ref, own_y - 1)):
                    ref[first // OV, k : k + 1, :columns] = result[first + k, at : at + 1]
                    ref[first // OV, k : k + 1, columns:] = extra_ref[first + k, at : at + 1]
    for send in sends:
        send.wait()
    if not last:
        first_ref[0] = jnp.concatenate([result[0], extra_ref[0]], axis=1)
        last_ref[0] = jnp.concatenate([result[own_x - 1], extra_ref[own_x - 1]], axis=1)


def shape_of(shape, kind):
    return jax.ShapeDtypeStruct(shape, kind)


def on_device(rhs, conductivity, local_inverse, coarse_basis, coarse_inverse):
    own_x, own_y, columns = rhs.shape
    modes = coarse_basis.shape[2]
    span_x = own_x + 2 * OV
    span_y = own_y + 2 * OV
    local = span_x * span_y
    basis = jnp.transpose(coarse_basis, (0, 2, 1))
    heat = jnp.broadcast_to(conductivity[:, :, None], (own_x, own_y, LANES))

    def params(mebibytes):
        return pltpu.CompilerParams(vmem_limit_bytes=mebibytes * 2**20)

    group = 2 * OV if own_x % (2 * OV) == 0 else OV
    in_vmem = pl.BlockSpec(memory_space=pltpu.VMEM)
    in_hbm = pl.BlockSpec(memory_space=pltpu.HBM)

    members, groups = lax.axis_size("mem"), lax.axis_size("grp")
    width = members * modes
    edge_rows = OV * own_y
    sum_rows = 2 * modes
    inverse_rows = 3 * width // columns * modes

    def survey_shapes(rows):
        return [
            shape_of((rows, columns), BF16),
            shape_of((rows, columns), BF16),
            shape_of((own_x, 2 * OV, columns), BF16),
            shape_of((modes, columns), F32),
        ]

    def surveyed_start():
        return pl.pallas_call(
            start_kernel,
            in_specs=[in_hbm] * 3,
            out_specs=[in_vmem] * 4,
            out_shape=survey_shapes(edge_rows + sum_rows + inverse_rows),
            scratch_shapes=[
                pltpu.VMEM(rhs.shape, F32),
                pltpu.VMEM(basis.shape, F32),
                pltpu.VMEM(coarse_inverse.shape, F32),
                pltpu.SemaphoreType.DMA((own_x // OV,)),
                pltpu.SemaphoreType.DMA((2,)),
            ],
            compiler_params=params(16),
        )(*(pltpu.with_memory_space_constraint(a, pltpu.HBM) for a in (rhs, basis, coarse_inverse)))

    edge_cells = 2 * own_y + 2 * OV * own_x

    def inner(now):
        return pl.pallas_call(
            inner_kernel,
            in_specs=[in_vmem] * 4,
            out_specs=[in_vmem] * 3,
            out_shape=[
                shape_of(rhs.shape, F32),
                shape_of((modes, columns), F32),
                shape_of((modes, edge_cells), F32),
            ],
            compiler_params=params(16),
            cost_estimate=pl.CostEstimate(
                flops=0, bytes_accessed=12 * own_x * own_y * columns, transcendentals=0
            ),
        )(rhs, now, heat, basis)

    def surveyed_residual(now, around):
        part, part_sum, edge_modes = inner(now)
        return pl.pallas_call(
            edge_kernel,
            in_specs=[in_vmem] * 9,
            out_specs=[in_vmem] * 5,
            out_shape=[shape_of(rhs.shape, F32)] + survey_shapes(edge_rows + sum_rows),
            scratch_shapes=[pltpu.VMEM((edge_cells, columns), F32)],
            input_output_aliases={0: 0},
            compiler_params=params(16),
        )(part, now, *around, heat, part_sum, edge_modes)

    def added(parts):
        return sum(part.astype(F32) for part in parts)

    def sums_in(message):
        return added(jnp.split(message[edge_rows : edge_rows + sum_rows], 2, axis=0))

    def inverse_in(message):
        pieces = message[edge_rows + sum_rows :]
        pieces = jnp.concatenate(jnp.split(pieces, inverse_rows // modes, axis=0), axis=1)
        return added(jnp.split(pieces, 3, axis=1))

    def inverse_for(distance):
        group = (lax.axis_index("grp") + distance) % groups
        return lax.dynamic_slice_in_dim(coarse_inverse, group * width, width, 1)

    def exchanged(down, up, sides, restricted, inverse):
        first = inverse is None
        from_below, from_above = shifted(up, "grp", 1), shifted(down, "grp", -1)
        sums = [restricted]
        rows = [inverse_for(0)]
        for distance in range(2, groups - 1):
            if first:
                message = jnp.concatenate([restricted, inverse_for(distance)], axis=1)
            else:
                message = restricted
            message = shifted(message, "grp", distance)
            sums.append(message[:, :columns])
            rows.append(message[:, columns:])
        for message in (from_below, from_above):
            sums.append(sums_in(message))
            if first:
                rows.append(inverse_in(message))
        if first:
            inverse = jnp.concatenate(rows, axis=0)
        low, high = beyond(from_below[:edge_rows], from_above[:edge_rows], "grp")
        low = low.reshape(OV, own_y, columns)
        high = high.reshape(OV, own_y, columns)
        corners = [jnp.concatenate([m[:, :OV], m[:, -OV:]], axis=1) for m in (low, high)]
        sides = jnp.concatenate([corners[0], sides, corners[1]], axis=0)
        left, right = edges(sides[:, :OV], sides[:, OV:], "mem")
        margins = low, high, jnp.concatenate([left, right], axis=1)
        return margins, jnp.concatenate(sums, axis=0), inverse

    def coarse_solve(inverse, sums):
        shares = lax.dot_general(
            inverse,
            sums,
            (((0,), (0,)), ((), ())),
            precision=EXACT,
            preferred_element_type=F32,
        )
        return summed_over_members(shares)

    held = (own_x * span_y, local)

    def held_rows(order):
        return pl.pallas_call(
            hold_kernel,
            in_specs=[in_hbm, pl.BlockSpec(memory_space=pl.ANY), pl.BlockSpec(memory_space=pl.ANY)],
            out_specs=in_vmem,
            out_shape=shape_of(held, BF16),
            scratch_shapes=[pltpu.SemaphoreType.DMA((own_x // OV,))],
            compiler_params=params(8),
            cost_estimate=pl.CostEstimate(
                flops=0, bytes_accessed=4 * held[0] * local, transcendentals=0
            ),
        )(pltpu.with_memory_space_constraint(local_inverse, pltpu.HBM), heat, order)

    def fine(rows, values, margins):
        return pl.pallas_call(
            fine_kernel,
            in_specs=[in_vmem] * 5,
            out_specs=in_vmem,
            out_shape=shape_of(rhs.shape, F32),
            scratch_shapes=[
                pltpu.VMEM((local, columns), BF16),
                pltpu.VMEM((span_y, columns), F32),
                pltpu.VMEM((group * span_y, columns), F32),
            ],
            compiler_params=params(24),
            cost_estimate=pl.CostEstimate(
                flops=2 * held[0] * local * columns,
                bytes_accessed=2 * held[0] * local,
                transcendentals=0,
            ),
        )(rows, values, *margins)

    def updated(solved, lifted, now):
        last = now is not None
        edge = columns + LANES
        out_shape = [shape_of(rhs.shape, F32)]
        if last:
            out_specs = [in_hbm]
            scratch = [pltpu.VMEM(rhs.shape, F32), pltpu.SemaphoreType.DMA((own_x // OV,))]
        else:
            out_specs = [in_vmem] * 5
            out_shape += [shape_of((1, own_y, edge), F32)] * 2
            out_shape += [shape_of((own_x // OV, OV, edge), F32)] * 2
            scratch = []
        return pl.pallas_call(
            functools.partial(update_kernel, last),
            in_specs=[in_vmem] * 4,
            out_specs=out_specs,
            out_shape=out_shape,
            scratch_shapes=scratch,
            compiler_params=params(16),
        )(solved, basis, lifted, now if last else heat)

    found = surveyed_start()
    rows = held_rows(found[-1])
    margins, sums, inverse = exchanged(*found, None)
    solved = fine(rows, rhs, margins)
    lifted = coarse_solve(inverse, sums)
    now, first, final, left, right = updated(solved, lifted, None)
    for sweep in range(ITERS - 1):
        around = edges(first, final, "grp") + edges(left, right, "mem")
        residual, *found = surveyed_residual(now, around)
        margins, sums, inverse = exchanged(*found, inverse)
        solved = fine(rows, residual, margins)
        lifted = coarse_solve(inverse, sums)
        now = updated(solved, lifted, now)[0]
    return now


def solution(mesh):
    placed = (
        P("grp", "mem", None),
        P("grp", "mem"),
        P(("grp", "mem"), None),
        P("grp", "mem", None),
        P(("grp", "mem"), None),
    )
    return jax.shard_map(
        on_device, mesh=mesh, in_specs=placed, out_specs=P("grp", "mem", None), check_vma=False
    )
```

```python
import functools

import jax
import jax.numpy as jnp
from jax import lax
from jax.experimental import pallas as pl
from jax.experimental.pallas import tpu as pltpu
from jax.sharding import PartitionSpec as P

OV = 4
ITERS = 2
LANES = 128
F32 = jnp.float32
BF16 = jnp.bfloat16


def shifted(value, axis, distance):
    count = lax.axis_size(axis)
    return lax.ppermute(value, axis, [(i, (i + distance) % count) for i in range(count)])


def edges(low_edge, high_edge, axis):
    return beyond(shifted(high_edge, axis, 1), shifted(low_edge, axis, -1), axis)


def beyond(low, high, axis):
    index = lax.axis_index(axis)
    last = lax.axis_size(axis) - 1
    return jnp.where(index == 0, 0, low), jnp.where(index == last, 0, high)


def summed_over_members(shares):
    members = lax.axis_size("mem")
    sizes = [2] * (members.bit_length() - 1)
    shares = shares.reshape(*sizes, shares.shape[0] // members, shares.shape[1])
    for k in (*range(1, len(sizes)), 0):
        bit = lax.axis_index("mem") >> k & 1
        axis = len(sizes) - 1 - k
        keep = lax.dynamic_slice_in_dim(shares, bit, 1, axis)
        send = lax.dynamic_slice_in_dim(shares, 1 - bit, 1, axis)
        pairs = [(i, i ^ 1 << k) for i in range(members)]
        shares = keep + lax.ppermute(send, "mem", pairs)
    return shares.reshape(shares.shape[-2:])


def split(values):
    high = values.astype(BF16)
    rest = values - high.astype(F32)
    middle = rest.astype(BF16)
    return high, middle, (rest - middle.astype(F32)).astype(BF16)


def product(a, b):
    return jnp.dot(a, b, preferred_element_type=F32)


def modes_of(basis_ref, first, rows):
    return split(jnp.concatenate([basis_ref[first + k] for k in range(rows)], axis=1))


def restrict(basis_ref, first, block):
    rows, own_y, columns = block.shape
    return weighted(modes_of(basis_ref, first, rows), block.reshape(rows * own_y, columns))


def weighted(weights, cells):
    high, middle, _ = weights
    modes = high.shape[0]
    cells_high = cells.astype(BF16)
    cells_middle = (cells - cells_high.astype(F32)).astype(BF16)
    two = product(jnp.concatenate([high, middle], axis=0), cells_high)
    return (product(high, cells_middle) + two[modes:]) + two[:modes]


def survey(block, basis_ref, first, down_ref, up_ref, side_ref):
    rows, own_y, columns = block.shape
    count = OV * own_y
    if first == 0:
        down_ref[:count] = block[:OV].reshape(count, columns).astype(BF16)
    if first + rows == side_ref.shape[0]:
        up_ref[:count] = block[rows - OV :].reshape(count, columns).astype(BF16)
    left = lax.broadcasted_iota(jnp.int32, (rows, 2 * OV, columns), 1) < OV
    side_ref[first : first + rows] = jnp.where(
        left, block[:, : 2 * OV], block[:, own_y - 2 * OV :]
    ).astype(BF16)
    return restrict(basis_ref, first, block)


def finish(total, start, down_ref, up_ref, sum_ref):
    sum_ref[...] = total
    parts = jnp.concatenate(split(total)[:2], axis=0)
    end = start + parts.shape[0]
    down_ref[start:end] = parts
    up_ref[start:end] = parts


def start_kernel(
    rhs_ref,
    basis_hbm,
    inverse_hbm,
    down_ref,
    up_ref,
    side_ref,
    sum_ref,
    held,
    basis_ref,
    inverse_ref,
    arrived,
    beside,
):
    own_x, own_y, columns = held.shape
    small = [
        pltpu.make_async_copy(inverse_hbm, inverse_ref, beside.at[0]),
        pltpu.make_async_copy(basis_hbm, basis_ref, beside.at[1]),
    ]
    copies = [
        pltpu.make_async_copy(
            rhs_ref.at[pl.ds(first, OV)], held.at[pl.ds(first, OV)], arrived.at[first // OV]
        )
        for first in range(0, own_x, OV)
    ]
    for copy in small + copies:
        copy.start()
    for copy in small:
        copy.wait()

    groups = lax.axis_size("grp")
    width = inverse_ref.shape[1] // groups
    modes = inverse_ref.shape[0]
    start = OV * own_y + 2 * modes
    for ref, step in ((up_ref, 1), (down_ref, groups - 1)):
        group = lax.rem(lax.axis_index("grp") + step, groups)
        wanted = inverse_ref[:, pl.ds(pl.multiple_of(group * width, width), width)]
        parts = jnp.concatenate(split(wanted), axis=1)
        for k in range(3 * width // columns):
            ref[start + k * modes : start + (k + 1) * modes] = parts[
                :, k * columns : (k + 1) * columns
            ]

    total = jnp.zeros(sum_ref.shape, F32)
    for first in range(0, own_x, OV):
        copies[first // OV].wait()
        block = held[first : first + OV]
        total = total + survey(block, basis_ref, first, down_ref, up_ref, side_ref)
    finish(total, OV * own_y, down_ref, up_ref, sum_ref)


def flux(values, heat, other, other_heat):
    face = 0.5 * (heat + other_heat)
    return jnp.concatenate([face] * (values.shape[1] // LANES), axis=1) * (values - other)


def inner_kernel(rhs_ref, now_ref, heat_ref, basis_ref, out_ref, sum_ref, modes_ref):
    own_x, own_y, columns = now_ref.shape
    place = lax.broadcasted_iota(jnp.int32, (own_y, columns), 0)
    here, heat = now_ref[0], heat_ref[0]
    before = jnp.zeros((own_y, columns), F32)
    total = jnp.zeros(sum_ref.shape, F32)
    for index in range(own_x):
        if index + 1 < own_x:
            after, after_heat = now_ref[index + 1], heat_ref[index + 1]
            across = flux(here, heat, after, after_heat)
        else:
            across = jnp.zeros((own_y, columns), F32)
        along = flux(here, heat, pltpu.roll(here, own_y - 1, 0), pltpu.roll(heat, own_y - 1, 0))
        along = jnp.where(place == own_y - 1, 0.0, along)
        entering = pltpu.roll(along, 1, 0)
        out_ref[index] = rhs_ref[index] - ((across - before) + (along - entering))
        here, heat, before = after, after_heat, across
        if index % OV == OV - 1:
            first = index + 1 - OV
            total = total + restrict(basis_ref, first, out_ref[first : first + OV])
    sum_ref[...] = total
    sides = []
    for index in range(own_x):
        row = basis_ref[index]
        left = lax.broadcasted_iota(jnp.int32, (row.shape[0], 2 * OV), 1) < OV
        sides.append(jnp.where(left, row[:, : 2 * OV], row[:, own_y - 2 * OV :]))
    modes_ref[...] = jnp.concatenate([basis_ref[0], basis_ref[own_x - 1], *sides], axis=1)


def edge_kernel(
    part_ref,
    now_ref,
    below_ref,
    above_ref,
    left_ref,
    right_ref,
    heat_ref,
    part_sum_ref,
    modes_ref,
    out_ref,
    down_ref,
    up_ref,
    side_ref,
    sum_ref,
    changes,
):
    del part_ref
    own_x, own_y, columns = now_ref.shape
    count = OV * own_y
    sides = 2 * OV

    def parts(row):
        return row[:, :columns], row[:, columns:]

    for at, index, ref in ((0, 0, below_ref), (own_y, own_x - 1, above_ref)):
        change = flux(*parts(ref[0]), now_ref[index], heat_ref[index])
        changes[at : at + own_y] = change
        out_ref[index] = out_ref[index] + change
    place = lax.broadcasted_iota(jnp.int32, (sides, columns), 0)
    for index in range(own_x):
        tiles = []
        for ref, start, cell in ((left_ref, 0, 0), (right_ref, own_y - sides, sides - 1)):
            other = parts(ref[index // OV, index % OV : index % OV + 1])
            tile = slice(start, start + sides)
            change = flux(*other, now_ref[index, tile], heat_ref[index, tile])
            change = jnp.where(place == cell, change, 0.0)
            tiles.append(change)
            out_ref[index, tile] = out_ref[index, tile] + change
        at = 2 * own_y + index * sides
        changes[at : at + sides] = tiles[0] + tiles[1]
        side_ref[index] = jnp.where(
            place < OV, out_ref[index, :sides], out_ref[index, own_y - sides :]
        ).astype(BF16)
    down_ref[:count] = out_ref[:OV].reshape(count, columns).astype(BF16)
    up_ref[:count] = out_ref[own_x - OV :].reshape(count, columns).astype(BF16)
    total = part_sum_ref[...] + weighted(split(modes_ref[...]), changes[...])
    finish(total, count, down_ref, up_ref, sum_ref)


def hold_kernel(inverse_ref, heat_ref, order_ref, out_ref, arrived):
    del heat_ref, order_ref
    count = arrived.shape[0]
    rows = out_ref.shape[0] // count
    skipped = (inverse_ref.shape[0] - out_ref.shape[0]) // 2
    copies = [
        pltpu.make_async_copy(
            inverse_ref.at[pl.ds(skipped + k * rows, rows)],
            out_ref.at[pl.ds(k * rows, rows)],
            arrived.at[k],
        )
        for k in range(count)
    ]
    for copy in copies:
        copy.start()
    for copy in copies:
        copy.wait()


def fine_kernel(rows_ref, block_ref, low_ref, high_ref, side_ref, out_ref, window, wide, solved):
    own_x, own_y, columns = block_ref.shape
    span_y = own_y + 2 * OV
    rows = solved.shape[0] // span_y

    def place(index, values):
        wide[OV : OV + own_y, :] = values
        sides = side_ref[index].astype(F32)
        wide[:OV, :] = sides[:OV]
        wide[OV + own_y :, :] = sides[OV:]
        window[index * span_y : (index + 1) * span_y, :] = wide[...].astype(BF16)

    for index in range(OV):
        place(index, low_ref[index].astype(F32))
        place(OV + own_x + index, high_ref[index].astype(F32))
    for index in range(own_x):
        place(OV + index, block_ref[index])

    for first in range(0, own_x, rows):
        solved[...] = product(
            rows_ref[first * span_y : (first + rows) * span_y, :], window[...]
        )
        for k in range(rows):
            out_ref[first + k] = solved[k * span_y + OV : k * span_y + OV + own_y, :]


def update_kernel(last, fine_ref, basis_ref, lifted_ref, extra_ref, out_ref, *refs):
    own_x, own_y, columns = fine_ref.shape
    if last:
        result, left_for = refs
    else:
        first_ref, last_ref, left_ref, right_ref = refs
        result = out_ref
    high, middle, low = split(lifted_ref[...])
    lifted = jnp.concatenate([high, middle, high, low, middle, high], axis=0)
    sends = []
    for first in range(0, own_x, OV):
        high, middle, low = modes_of(basis_ref, first, OV)
        coarse = lax.dot_general(
            jnp.concatenate([high, high, middle, high, middle, low], axis=0),
            lifted,
            (((0,), (0,)), ((), ())),
            preferred_element_type=F32,
        )
        for k in range(OV):
            value = fine_ref[first + k] + coarse[k * own_y : (k + 1) * own_y]
            if last:
                value = extra_ref[first + k] + value
            result[first + k] = value
        if last:
            sends.append(
                pltpu.make_async_copy(
                    result.at[pl.ds(first, OV)],
                    out_ref.at[pl.ds(first, OV)],
                    left_for.at[first // OV],
                )
            )
            sends[-1].start()
        else:
            for k in range(OV):
                for ref, at in ((left_ref, 0), (right_ref, own_y - 1)):
                    ref[first // OV, k : k + 1, :columns] = result[first + k, at : at + 1]
                    ref[first // OV, k : k + 1, columns:] = extra_ref[first + k, at : at + 1]
    for send in sends:
        send.wait()
    if not last:
        first_ref[0] = jnp.concatenate([result[0], extra_ref[0]], axis=1)
        last_ref[0] = jnp.concatenate([result[own_x - 1], extra_ref[own_x - 1]], axis=1)


def shape_of(shape, kind):
    return jax.ShapeDtypeStruct(shape, kind)


def on_device(rhs, conductivity, local_inverse, coarse_basis, coarse_inverse):
    own_x, own_y, columns = rhs.shape
    modes = coarse_basis.shape[2]
    span_x = own_x + 2 * OV
    span_y = own_y + 2 * OV
    local = span_x * span_y
    basis = jnp.transpose(coarse_basis, (0, 2, 1))
    heat = jnp.broadcast_to(conductivity[:, :, None], (own_x, own_y, LANES))

    def params(mebibytes):
        return pltpu.CompilerParams(vmem_limit_bytes=mebibytes * 2**20)

    group = 2 * OV if own_x % (2 * OV) == 0 else OV
    in_vmem = pl.BlockSpec(memory_space=pltpu.VMEM)
    in_hbm = pl.BlockSpec(memory_space=pltpu.HBM)

    members, groups = lax.axis_size("mem"), lax.axis_size("grp")
    width = members * modes
    edge_rows = OV * own_y
    sum_rows = 2 * modes
    inverse_rows = 3 * width // columns * modes

    def survey_shapes(rows):
        return [
            shape_of((rows, columns), BF16),
            shape_of((rows, columns), BF16),
            shape_of((own_x, 2 * OV, columns), BF16),
            shape_of((modes, columns), F32),
        ]

    def surveyed_start():
        return pl.pallas_call(
            start_kernel,
            in_specs=[in_hbm] * 3,
            out_specs=[in_vmem] * 4,
            out_shape=survey_shapes(edge_rows + sum_rows + inverse_rows),
            scratch_shapes=[
                pltpu.VMEM(rhs.shape, F32),
                pltpu.VMEM(basis.shape, F32),
                pltpu.VMEM(coarse_inverse.shape, F32),
                pltpu.SemaphoreType.DMA((own_x // OV,)),
                pltpu.SemaphoreType.DMA((2,)),
            ],
            compiler_params=params(16),
        )(*(pltpu.with_memory_space_constraint(a, pltpu.HBM) for a in (rhs, basis, coarse_inverse)))

    edge_cells = 2 * own_y + 2 * OV * own_x

    def inner(now):
        return pl.pallas_call(
            inner_kernel,
            in_specs=[in_vmem] * 4,
            out_specs=[in_vmem] * 3,
            out_shape=[
                shape_of(rhs.shape, F32),
                shape_of((modes, columns), F32),
                shape_of((modes, edge_cells), F32),
            ],
            compiler_params=params(16),
            cost_estimate=pl.CostEstimate(
                flops=0, bytes_accessed=12 * own_x * own_y * columns, transcendentals=0
            ),
        )(rhs, now, heat, basis)

    def surveyed_residual(now, around):
        part, part_sum, edge_modes = inner(now)
        return pl.pallas_call(
            edge_kernel,
            in_specs=[in_vmem] * 9,
            out_specs=[in_vmem] * 5,
            out_shape=[shape_of(rhs.shape, F32)] + survey_shapes(edge_rows + sum_rows),
            scratch_shapes=[pltpu.VMEM((edge_cells, columns), F32)],
            input_output_aliases={0: 0},
            compiler_params=params(16),
        )(part, now, *around, heat, part_sum, edge_modes)

    def added(parts):
        return sum(part.astype(F32) for part in parts)

    def sums_in(message):
        return added(jnp.split(message[edge_rows : edge_rows + sum_rows], 2, axis=0))

    def inverse_in(message):
        pieces = message[edge_rows + sum_rows :]
        pieces = jnp.concatenate(jnp.split(pieces, inverse_rows // modes, axis=0), axis=1)
        return added(jnp.split(pieces, 3, axis=1))

    def inverse_for(distance):
        group = (lax.axis_index("grp") + distance) % groups
        return lax.dynamic_slice_in_dim(coarse_inverse, group * width, width, 1)

    def exchanged(down, up, sides, restricted, inverse):
        first = inverse is None
        from_below, from_above = shifted(up, "grp", 1), shifted(down, "grp", -1)
        sums = [restricted]
        rows = [inverse_for(0)]
        for distance in range(2, groups - 1):
            if first:
                message = jnp.concatenate([restricted, inverse_for(distance)], axis=1)
            else:
                message = restricted
            message = shifted(message, "grp", distance)
            sums.append(message[:, :columns])
            rows.append(message[:, columns:])
        for message in (from_below, from_above):
            sums.append(sums_in(message))
            if first:
                rows.append(inverse_in(message))
        if first:
            inverse = jnp.concatenate(rows, axis=0)
        low, high = beyond(from_below[:edge_rows], from_above[:edge_rows], "grp")
        low = low.reshape(OV, own_y, columns)
        high = high.reshape(OV, own_y, columns)
        corners = [jnp.concatenate([m[:, :OV], m[:, -OV:]], axis=1) for m in (low, high)]
        sides = jnp.concatenate([corners[0], sides, corners[1]], axis=0)
        left, right = edges(sides[:, :OV], sides[:, OV:], "mem")
        margins = low, high, jnp.concatenate([left, right], axis=1)
        return margins, jnp.concatenate(sums, axis=0), inverse

    def coarse_solve(inverse, sums):
        shares = lax.dot_general(
            inverse,
            sums,
            (((0,), (0,)), ((), ())),
            precision=lax.Precision.HIGH,
            preferred_element_type=F32,
        )
        return summed_over_members(shares)

    held = (own_x * span_y, local)

    def held_rows(order):
        return pl.pallas_call(
            hold_kernel,
            in_specs=[in_hbm, pl.BlockSpec(memory_space=pl.ANY), pl.BlockSpec(memory_space=pl.ANY)],
            out_specs=in_vmem,
            out_shape=shape_of(held, BF16),
            scratch_shapes=[pltpu.SemaphoreType.DMA((own_x // OV,))],
            compiler_params=params(8),
            cost_estimate=pl.CostEstimate(
                flops=0, bytes_accessed=4 * held[0] * local, transcendentals=0
            ),
        )(pltpu.with_memory_space_constraint(local_inverse, pltpu.HBM), heat, order)

    def fine(rows, values, margins):
        return pl.pallas_call(
            fine_kernel,
            in_specs=[in_vmem] * 5,
            out_specs=in_vmem,
            out_shape=shape_of(rhs.shape, F32),
            scratch_shapes=[
                pltpu.VMEM((local, columns), BF16),
                pltpu.VMEM((span_y, columns), F32),
                pltpu.VMEM((group * span_y, columns), F32),
            ],
            compiler_params=params(24),
            cost_estimate=pl.CostEstimate(
                flops=2 * held[0] * local * columns,
                bytes_accessed=2 * held[0] * local,
                transcendentals=0,
            ),
        )(rows, values, *margins)

    def updated(solved, lifted, now):
        last = now is not None
        edge = columns + LANES
        out_shape = [shape_of(rhs.shape, F32)]
        if last:
            out_specs = [in_hbm]
            scratch = [pltpu.VMEM(rhs.shape, F32), pltpu.SemaphoreType.DMA((own_x // OV,))]
        else:
            out_specs = [in_vmem] * 5
            out_shape += [shape_of((1, own_y, edge), F32)] * 2
            out_shape += [shape_of((own_x // OV, OV, edge), F32)] * 2
            scratch = []
        return pl.pallas_call(
            functools.partial(update_kernel, last),
            in_specs=[in_vmem] * 4,
            out_specs=out_specs,
            out_shape=out_shape,
            scratch_shapes=scratch,
            compiler_params=params(16),
        )(solved, basis, lifted, now if last else heat)

    found = surveyed_start()
    rows = held_rows(found[-1])
    margins, sums, inverse = exchanged(*found, None)
    solved = fine(rows, rhs, margins)
    lifted = coarse_solve(inverse, sums)
    now, first, final, left, right = updated(solved, lifted, None)
    for sweep in range(ITERS - 1):
        around = edges(first, final, "grp") + edges(left, right, "mem")
        residual, *found = surveyed_residual(now, around)
        margins, sums, inverse = exchanged(*found, inverse)
        solved = fine(rows, residual, margins)
        lifted = coarse_solve(inverse, sums)
        now = updated(solved, lifted, now)[0]
    return now


def solution(mesh):
    placed = (
        P("grp", "mem", None),
        P("grp", "mem"),
        P(("grp", "mem"), None),
        P("grp", "mem", None),
        P(("grp", "mem"), None),
    )
    return jax.shard_map(
        on_device, mesh=mesh, in_specs=placed, out_specs=P("grp", "mem", None), check_vma=False
    )
```

```python
import functools

import jax
import jax.numpy as jnp
from jax import lax
from jax.experimental import pallas as pl
from jax.experimental.pallas import tpu as pltpu
from jax.sharding import PartitionSpec as P

OV = 4
ITERS = 2
LANES = 128
F32 = jnp.float32
BF16 = jnp.bfloat16


def shifted(value, axis, distance):
    count = lax.axis_size(axis)
    return lax.ppermute(value, axis, [(i, (i + distance) % count) for i in range(count)])


def edges(low_edge, high_edge, axis):
    return beyond(shifted(high_edge, axis, 1), shifted(low_edge, axis, -1), axis)


def beyond(low, high, axis):
    index = lax.axis_index(axis)
    last = lax.axis_size(axis) - 1
    return jnp.where(index == 0, 0, low), jnp.where(index == last, 0, high)


def summed_over_members(shares):
    members = lax.axis_size("mem")
    sizes = [2] * (members.bit_length() - 1)
    shares = shares.reshape(*sizes, shares.shape[0] // members, shares.shape[1])
    for k in (*range(1, len(sizes)), 0):
        bit = lax.axis_index("mem") >> k & 1
        axis = len(sizes) - 1 - k
        keep = lax.dynamic_slice_in_dim(shares, bit, 1, axis)
        send = lax.dynamic_slice_in_dim(shares, 1 - bit, 1, axis)
        pairs = [(i, i ^ 1 << k) for i in range(members)]
        shares = keep + lax.ppermute(send, "mem", pairs)
    return shares.reshape(shares.shape[-2:])


def split(values):
    high = values.astype(BF16)
    rest = values - high.astype(F32)
    middle = rest.astype(BF16)
    return high, middle, (rest - middle.astype(F32)).astype(BF16)


def product(a, b):
    return jnp.dot(a, b, preferred_element_type=F32)


def modes_of(basis_ref, first, rows):
    return split(jnp.concatenate([basis_ref[first + k] for k in range(rows)], axis=1))


def restrict(basis_ref, first, block):
    rows, own_y, columns = block.shape
    return weighted(modes_of(basis_ref, first, rows), block.reshape(rows * own_y, columns))


def weighted(weights, cells):
    high, middle, _ = weights
    modes = high.shape[0]
    cells_high = cells.astype(BF16)
    cells_middle = (cells - cells_high.astype(F32)).astype(BF16)
    two = product(jnp.concatenate([high, middle], axis=0), cells_high)
    return (product(high, cells_middle) + two[modes:]) + two[:modes]


def survey(block, basis_ref, first, down_ref, up_ref, side_ref):
    rows, own_y, columns = block.shape
    count = OV * own_y
    if first == 0:
        down_ref[:count] = block[:OV].reshape(count, columns).astype(BF16)
    if first + rows == side_ref.shape[0]:
        up_ref[:count] = block[rows - OV :].reshape(count, columns).astype(BF16)
    left = lax.broadcasted_iota(jnp.int32, (rows, 2 * OV, columns), 1) < OV
    side_ref[first : first + rows] = jnp.where(
        left, block[:, : 2 * OV], block[:, own_y - 2 * OV :]
    ).astype(BF16)
    return restrict(basis_ref, first, block)


def finish(total, start, down_ref, up_ref, sum_ref):
    sum_ref[...] = total
    parts = jnp.concatenate(split(total)[:2], axis=0)
    end = start + parts.shape[0]
    down_ref[start:end] = parts
    up_ref[start:end] = parts


def start_kernel(
    rhs_ref,
    basis_hbm,
    inverse_hbm,
    down_ref,
    up_ref,
    side_ref,
    sum_ref,
    held,
    basis_ref,
    inverse_ref,
    arrived,
    beside,
):
    own_x, own_y, columns = held.shape
    small = [
        pltpu.make_async_copy(inverse_hbm, inverse_ref, beside.at[0]),
        pltpu.make_async_copy(basis_hbm, basis_ref, beside.at[1]),
    ]
    copies = [
        pltpu.make_async_copy(
            rhs_ref.at[pl.ds(first, OV)], held.at[pl.ds(first, OV)], arrived.at[first // OV]
        )
        for first in range(0, own_x, OV)
    ]
    for copy in small + copies:
        copy.start()
    for copy in small:
        copy.wait()

    groups = lax.axis_size("grp")
    width = inverse_ref.shape[1] // groups
    modes = inverse_ref.shape[0]
    start = OV * own_y + 2 * modes
    for ref, step in ((up_ref, 1), (down_ref, groups - 1)):
        group = lax.rem(lax.axis_index("grp") + step, groups)
        wanted = inverse_ref[:, pl.ds(pl.multiple_of(group * width, width), width)]
        parts = jnp.concatenate(split(wanted), axis=1)
        for k in range(3 * width // columns):
            ref[start + k * modes : start + (k + 1) * modes] = parts[
                :, k * columns : (k + 1) * columns
            ]

    total = jnp.zeros(sum_ref.shape, F32)
    for first in range(0, own_x, OV):
        copies[first // OV].wait()
        block = held[first : first + OV]
        total = total + survey(block, basis_ref, first, down_ref, up_ref, side_ref)
    finish(total, OV * own_y, down_ref, up_ref, sum_ref)


def flux(values, heat, other, other_heat):
    face = 0.5 * (heat + other_heat)
    return jnp.concatenate([face] * (values.shape[1] // LANES), axis=1) * (values - other)


def inner_kernel(rhs_ref, now_ref, heat_ref, basis_ref, out_ref, sum_ref, modes_ref):
    own_x, own_y, columns = now_ref.shape
    place = lax.broadcasted_iota(jnp.int32, (own_y, columns), 0)
    here, heat = now_ref[0], heat_ref[0]
    before = jnp.zeros((own_y, columns), F32)
    total = jnp.zeros(sum_ref.shape, F32)
    for index in range(own_x):
        if index + 1 < own_x:
            after, after_heat = now_ref[index + 1], heat_ref[index + 1]
            across = flux(here, heat, after, after_heat)
        else:
            across = jnp.zeros((own_y, columns), F32)
        along = flux(here, heat, pltpu.roll(here, own_y - 1, 0), pltpu.roll(heat, own_y - 1, 0))
        along = jnp.where(place == own_y - 1, 0.0, along)
        entering = pltpu.roll(along, 1, 0)
        out_ref[index] = rhs_ref[index] - ((across - before) + (along - entering))
        here, heat, before = after, after_heat, across
        if index % OV == OV - 1:
            first = index + 1 - OV
            total = total + restrict(basis_ref, first, out_ref[first : first + OV])
    sum_ref[...] = total
    sides = []
    for index in range(own_x):
        row = basis_ref[index]
        left = lax.broadcasted_iota(jnp.int32, (row.shape[0], 2 * OV), 1) < OV
        sides.append(jnp.where(left, row[:, : 2 * OV], row[:, own_y - 2 * OV :]))
    modes_ref[...] = jnp.concatenate([basis_ref[0], basis_ref[own_x - 1], *sides], axis=1)


def edge_kernel(
    part_ref,
    now_ref,
    below_ref,
    above_ref,
    left_ref,
    right_ref,
    heat_ref,
    part_sum_ref,
    modes_ref,
    out_ref,
    down_ref,
    up_ref,
    side_ref,
    sum_ref,
    changes,
):
    del part_ref
    own_x, own_y, columns = now_ref.shape
    count = OV * own_y
    sides = 2 * OV

    def parts(row):
        return row[:, :columns], row[:, columns:]

    for at, index, ref in ((0, 0, below_ref), (own_y, own_x - 1, above_ref)):
        change = flux(*parts(ref[0]), now_ref[index], heat_ref[index])
        changes[at : at + own_y] = change
        out_ref[index] = out_ref[index] + change
    place = lax.broadcasted_iota(jnp.int32, (sides, columns), 0)
    for index in range(own_x):
        tiles = []
        for ref, start, cell in ((left_ref, 0, 0), (right_ref, own_y - sides, sides - 1)):
            other = parts(ref[index // OV, index % OV : index % OV + 1])
            tile = slice(start, start + sides)
            change = flux(*other, now_ref[index, tile], heat_ref[index, tile])
            change = jnp.where(place == cell, change, 0.0)
            tiles.append(change)
            out_ref[index, tile] = out_ref[index, tile] + change
        at = 2 * own_y + index * sides
        changes[at : at + sides] = tiles[0] + tiles[1]
        side_ref[index] = jnp.where(
            place < OV, out_ref[index, :sides], out_ref[index, own_y - sides :]
        ).astype(BF16)
    down_ref[:count] = out_ref[:OV].reshape(count, columns).astype(BF16)
    up_ref[:count] = out_ref[own_x - OV :].reshape(count, columns).astype(BF16)
    total = part_sum_ref[...] + weighted(split(modes_ref[...]), changes[...])
    finish(total, count, down_ref, up_ref, sum_ref)


def hold_kernel(inverse_ref, heat_ref, order_ref, out_ref, arrived):
    del heat_ref, order_ref
    count = arrived.shape[0]
    rows = out_ref.shape[0] // count
    skipped = (inverse_ref.shape[0] - out_ref.shape[0]) // 2
    copies = [
        pltpu.make_async_copy(
            inverse_ref.at[pl.ds(skipped + k * rows, rows)],
            out_ref.at[pl.ds(k * rows, rows)],
            arrived.at[k],
        )
        for k in range(count)
    ]
    for copy in copies:
        copy.start()
    for copy in copies:
        copy.wait()


def fine_kernel(rows_ref, block_ref, low_ref, high_ref, side_ref, out_ref, window, wide, solved):
    own_x, own_y, columns = block_ref.shape
    span_y = own_y + 2 * OV
    rows = solved.shape[0] // span_y

    def place(index, values):
        wide[OV : OV + own_y, :] = values
        sides = side_ref[index].astype(F32)
        wide[:OV, :] = sides[:OV]
        wide[OV + own_y :, :] = sides[OV:]
        window[index * span_y : (index + 1) * span_y, :] = wide[...].astype(BF16)

    for index in range(OV):
        place(index, low_ref[index].astype(F32))
        place(OV + own_x + index, high_ref[index].astype(F32))
    for index in range(own_x):
        place(OV + index, block_ref[index])

    for first in range(0, own_x, rows):
        solved[...] = product(
            rows_ref[first * span_y : (first + rows) * span_y, :], window[...]
        )
        for k in range(rows):
            out_ref[first + k] = solved[k * span_y + OV : k * span_y + OV + own_y, :]


def update_kernel(last, fine_ref, basis_ref, lifted_ref, extra_ref, out_ref, *refs):
    own_x, own_y, columns = fine_ref.shape
    if last:
        result, left_for = refs
    else:
        first_ref, last_ref, left_ref, right_ref = refs
        result = out_ref
    high, middle, _ = split(lifted_ref[...])
    lifted = jnp.concatenate([high, middle, high], axis=0)
    sends = []
    for first in range(0, own_x, OV):
        high, middle, _ = modes_of(basis_ref, first, OV)
        coarse = lax.dot_general(
            jnp.concatenate([high, high, middle], axis=0),
            lifted,
            (((0,), (0,)), ((), ())),
            preferred_element_type=F32,
        )
        for k in range(OV):
            value = fine_ref[first + k] + coarse[k * own_y : (k + 1) * own_y]
            if last:
                value = extra_ref[first + k] + value
            result[first + k] = value
        if last:
            sends.append(
                pltpu.make_async_copy(
                    result.at[pl.ds(first, OV)],
                    out_ref.at[pl.ds(first, OV)],
                    left_for.at[first // OV],
                )
            )
            sends[-1].start()
        else:
            for k in range(OV):
                for ref, at in ((left_ref, 0), (right_ref, own_y - 1)):
                    ref[first // OV, k : k + 1, :columns] = result[first + k, at : at + 1]
                    ref[first // OV, k : k + 1, columns:] = extra_ref[first + k, at : at + 1]
    for send in sends:
        send.wait()
    if not last:
        first_ref[0] = jnp.concatenate([result[0], extra_ref[0]], axis=1)
        last_ref[0] = jnp.concatenate([result[own_x - 1], extra_ref[own_x - 1]], axis=1)


def shape_of(shape, kind):
    return jax.ShapeDtypeStruct(shape, kind)


def on_device(rhs, conductivity, local_inverse, coarse_basis, coarse_inverse):
    own_x, own_y, columns = rhs.shape
    modes = coarse_basis.shape[2]
    span_x = own_x + 2 * OV
    span_y = own_y + 2 * OV
    local = span_x * span_y
    basis = jnp.transpose(coarse_basis, (0, 2, 1))
    heat = jnp.broadcast_to(conductivity[:, :, None], (own_x, own_y, LANES))

    def params(mebibytes):
        return pltpu.CompilerParams(vmem_limit_bytes=mebibytes * 2**20)

    group = 2 * OV if own_x % (2 * OV) == 0 else OV
    in_vmem = pl.BlockSpec(memory_space=pltpu.VMEM)
    in_hbm = pl.BlockSpec(memory_space=pltpu.HBM)

    members, groups = lax.axis_size("mem"), lax.axis_size("grp")
    width = members * modes
    edge_rows = OV * own_y
    sum_rows = 2 * modes
    inverse_rows = 3 * width // columns * modes

    def survey_shapes(rows):
        return [
            shape_of((rows, columns), BF16),
            shape_of((rows, columns), BF16),
            shape_of((own_x, 2 * OV, columns), BF16),
            shape_of((modes, columns), F32),
        ]

    def surveyed_start():
        return pl.pallas_call(
            start_kernel,
            in_specs=[in_hbm] * 3,
            out_specs=[in_vmem] * 4,
            out_shape=survey_shapes(edge_rows + sum_rows + inverse_rows),
            scratch_shapes=[
                pltpu.VMEM(rhs.shape, F32),
                pltpu.VMEM(basis.shape, F32),
                pltpu.VMEM(coarse_inverse.shape, F32),
                pltpu.SemaphoreType.DMA((own_x // OV,)),
                pltpu.SemaphoreType.DMA((2,)),
            ],
            compiler_params=params(16),
        )(*(pltpu.with_memory_space_constraint(a, pltpu.HBM) for a in (rhs, basis, coarse_inverse)))

    edge_cells = 2 * own_y + 2 * OV * own_x

    def inner(now):
        return pl.pallas_call(
            inner_kernel,
            in_specs=[in_vmem] * 4,
            out_specs=[in_vmem] * 3,
            out_shape=[
                shape_of(rhs.shape, F32),
                shape_of((modes, columns), F32),
                shape_of((modes, edge_cells), F32),
            ],
            compiler_params=params(16),
            cost_estimate=pl.CostEstimate(
                flops=0, bytes_accessed=12 * own_x * own_y * columns, transcendentals=0
            ),
        )(rhs, now, heat, basis)

    def surveyed_residual(now, around):
        part, part_sum, edge_modes = inner(now)
        return pl.pallas_call(
            edge_kernel,
            in_specs=[in_vmem] * 9,
            out_specs=[in_vmem] * 5,
            out_shape=[shape_of(rhs.shape, F32)] + survey_shapes(edge_rows + sum_rows),
            scratch_shapes=[pltpu.VMEM((edge_cells, columns), F32)],
            input_output_aliases={0: 0},
            compiler_params=params(16),
        )(part, now, *around, heat, part_sum, edge_modes)

    def added(parts):
        return sum(part.astype(F32) for part in parts)

    def sums_in(message):
        return added(jnp.split(message[edge_rows : edge_rows + sum_rows], 2, axis=0))

    def inverse_in(message):
        pieces = message[edge_rows + sum_rows :]
        pieces = jnp.concatenate(jnp.split(pieces, inverse_rows // modes, axis=0), axis=1)
        return added(jnp.split(pieces, 3, axis=1))

    def inverse_for(distance):
        group = (lax.axis_index("grp") + distance) % groups
        return lax.dynamic_slice_in_dim(coarse_inverse, group * width, width, 1)

    def exchanged(down, up, sides, restricted, inverse):
        first = inverse is None
        from_below, from_above = shifted(up, "grp", 1), shifted(down, "grp", -1)
        sums = [restricted]
        rows = [inverse_for(0)]
        for distance in range(2, groups - 1):
            if first:
                message = jnp.concatenate([restricted, inverse_for(distance)], axis=1)
            else:
                message = restricted
            message = shifted(message, "grp", distance)
            sums.append(message[:, :columns])
            rows.append(message[:, columns:])
        for message in (from_below, from_above):
            sums.append(sums_in(message))
            if first:
                rows.append(inverse_in(message))
        if first:
            inverse = jnp.concatenate(rows, axis=0)
        low, high = beyond(from_below[:edge_rows], from_above[:edge_rows], "grp")
        low = low.reshape(OV, own_y, columns)
        high = high.reshape(OV, own_y, columns)
        corners = [jnp.concatenate([m[:, :OV], m[:, -OV:]], axis=1) for m in (low, high)]
        sides = jnp.concatenate([corners[0], sides, corners[1]], axis=0)
        left, right = edges(sides[:, :OV], sides[:, OV:], "mem")
        margins = low, high, jnp.concatenate([left, right], axis=1)
        return margins, jnp.concatenate(sums, axis=0), inverse

    def coarse_solve(inverse, sums):
        shares = lax.dot_general(
            inverse,
            sums,
            (((0,), (0,)), ((), ())),
            precision=lax.Precision.HIGH,
            preferred_element_type=F32,
        )
        return summed_over_members(shares)

    held = (own_x * span_y, local)

    def held_rows(order):
        return pl.pallas_call(
            hold_kernel,
            in_specs=[in_hbm, pl.BlockSpec(memory_space=pl.ANY), pl.BlockSpec(memory_space=pl.ANY)],
            out_specs=in_vmem,
            out_shape=shape_of(held, BF16),
            scratch_shapes=[pltpu.SemaphoreType.DMA((own_x // OV,))],
            compiler_params=params(8),
            cost_estimate=pl.CostEstimate(
                flops=0, bytes_accessed=4 * held[0] * local, transcendentals=0
            ),
        )(pltpu.with_memory_space_constraint(local_inverse, pltpu.HBM), heat, order)

    def fine(rows, values, margins):
        return pl.pallas_call(
            fine_kernel,
            in_specs=[in_vmem] * 5,
            out_specs=in_vmem,
            out_shape=shape_of(rhs.shape, F32),
            scratch_shapes=[
                pltpu.VMEM((local, columns), BF16),
                pltpu.VMEM((span_y, columns), F32),
                pltpu.VMEM((group * span_y, columns), F32),
            ],
            compiler_params=params(24),
            cost_estimate=pl.CostEstimate(
                flops=2 * held[0] * local * columns,
                bytes_accessed=2 * held[0] * local,
                transcendentals=0,
            ),
        )(rows, values, *margins)

    def updated(solved, lifted, now):
        last = now is not None
        edge = columns + LANES
        out_shape = [shape_of(rhs.shape, F32)]
        if last:
            out_specs = [in_hbm]
            scratch = [pltpu.VMEM(rhs.shape, F32), pltpu.SemaphoreType.DMA((own_x // OV,))]
        else:
            out_specs = [in_vmem] * 5
            out_shape += [shape_of((1, own_y, edge), F32)] * 2
            out_shape += [shape_of((own_x // OV, OV, edge), F32)] * 2
            scratch = []
        return pl.pallas_call(
            functools.partial(update_kernel, last),
            in_specs=[in_vmem] * 4,
            out_specs=out_specs,
            out_shape=out_shape,
            scratch_shapes=scratch,
            compiler_params=params(16),
        )(solved, basis, lifted, now if last else heat)

    found = surveyed_start()
    rows = held_rows(found[-1])
    margins, sums, inverse = exchanged(*found, None)
    solved = fine(rows, rhs, margins)
    lifted = coarse_solve(inverse, sums)
    now, first, final, left, right = updated(solved, lifted, None)
    for sweep in range(ITERS - 1):
        around = edges(first, final, "grp") + edges(left, right, "mem")
        residual, *found = surveyed_residual(now, around)
        margins, sums, inverse = exchanged(*found, inverse)
        solved = fine(rows, residual, margins)
        lifted = coarse_solve(inverse, sums)
        now = updated(solved, lifted, now)[0]
    return now


def solution(mesh):
    placed = (
        P("grp", "mem", None),
        P("grp", "mem"),
        P(("grp", "mem"), None),
        P("grp", "mem", None),
        P(("grp", "mem"), None),
    )
    return jax.shard_map(
        on_device, mesh=mesh, in_specs=placed, out_specs=P("grp", "mem", None), check_vma=False
    )
```
